256 devices in a mesh: frame: 8 (over z), row: 32 (over x, y, core).
Axes of the slice: x: 4, y: 4, z: 8, core: 2. Of those that a mesh axis runs over, the one named last changes fastest.
Arguments:
- inputs: bfloat16 [64, 128, 128, 256], P('frame', 'row'), may hold values from -6 to 6
- temporal_weight: bfloat16 [3, 256, 256], replicated, may hold values from -0.21875 to 0.21875
- spatial_weight: bfloat16 [3, 3, 256, 256], replicated, may hold values from -0.125 to 0.125
- pooled_grad: bfloat16 [32, 128, 128, 256], P('frame', 'row'), may hold values from -6 to 6
Outputs:
- input_grad: bfloat16 [64, 128, 128, 256], P('frame', 'row')
- temporal_grad: float32 [3, 256, 256], replicated
- spatial_grad: float32 [3, 3, 256, 256], replicated
The draws below stay inside these ranges and needn't reach their ends.
All inputs are finite; a program needn't handle non-finite values.
Results may differ from the reference program's by a relative error of at most 0.0049.
Values may be sent and summed in bfloat16 or wider, within the bound.
A program may use at most 64 MiB of HBM per device.

```python
import jax
import jax.numpy as jnp
from jax import lax

C = 256
W = 128
FRAMES = 64
H = 128
TOKENS = 1048576


def shard_levels(own_key, dims, pieces, least, largest):
    def one(position, blocks):
        draws = jax.random.uniform(jax.random.fold_in(jax.random.fold_in(own_key, 6), position), (blocks,), jnp.float32, least / len(pieces), largest / len(pieces))
        return jnp.repeat(jnp.exp(draws), dims[position] // blocks).reshape((-1,) + (1,) * (len(dims) - position - 1))

    gain = one(*pieces[0])
    for cut in pieces[1:]:
        gain = gain * one(*cut)
    return gain


def noise(rng, extent, width, bound, shards=(), kind=jnp.bfloat16):
    gain = shard_levels(rng, extent, shards, -0.22, 0.18) if shards else 1.0
    values = jax.random.normal(rng, extent, jnp.float32) * width * gain
    return jnp.minimum(jnp.maximum(values, -bound), bound).astype(kind)


def setup_inputs(seed: int = 0) -> dict:
    arg_keys = jax.random.split(jax.random.key(seed), 5)
    return {
        "inputs": noise(arg_keys[0], (FRAMES, H, W, C), 1.0, 6.0, ((0, 8), (1, 32))),
        "temporal_weight": noise(arg_keys[1], (3, C, C), (3 * C) ** -0.5, 0.21875),
        "spatial_weight": noise(arg_keys[2], (3, 3, C, C), (9 * C) ** -0.5, 0.125),
        "pooled_grad": noise(arg_keys[3], (FRAMES // 2, H, W, C), 1.0, 6.0, ((0, 8), (1, 32))),
    }


def tdot(left, right):
    return lax.dot_general(left, right, (((0,), (0,)), ((), ())), preferred_element_type=jnp.float32)

def reference(inputs, temporal_weight, spatial_weight, pooled_grad):
    chans = inputs.shape[3]
    nframes = inputs.shape[0]
    padded = jnp.pad(inputs, ((1, 1), (0, 0), (0, 0), (0, 0)))
    mixed = jnp.zeros(inputs.shape, jnp.float32)
    for k in range(3):
        part = jnp.dot(padded[k:k + nframes].reshape(-1, chans), temporal_weight[k], preferred_element_type=jnp.float32)
        mixed = mixed + part.reshape(inputs.shape)
    features = (inputs.astype(jnp.float32) + mixed).astype(jnp.bfloat16)
    frame_grad = (jnp.repeat(pooled_grad, 2, axis=0).astype(jnp.float32) * 0.5).astype(jnp.bfloat16)

    def one_frame(carry, pair):
        feat, grad = pair
        fpad = jnp.pad(feat, ((1, 1), (1, 1), (0, 0)))
        gpad = jnp.pad(grad, ((1, 1), (1, 1), (0, 0)))
        flat = grad.reshape(-1, chans)
        terms = []
        back = jnp.zeros((H * W, chans), jnp.float32)
        for a in range(3):
            for b in range(3):
                terms.append(tdot(fpad[a:a + H, b:b + W].reshape(-1, chans), flat))
                back = back + jnp.dot(gpad[2 - a:2 - a + H, 2 - b:2 - b + W].reshape(-1, chans), spatial_weight[a, b].T, preferred_element_type=jnp.float32)
        return (carry + jnp.stack(terms).reshape(3, 3, chans, chans), back.astype(jnp.bfloat16).reshape(H, W, chans))
    spatial_sum, feature_grad = lax.scan(one_frame, jnp.zeros((3, 3, chans, chans), jnp.float32), (features, frame_grad))
    gpadded = jnp.pad(feature_grad, ((1, 1), (0, 0), (0, 0), (0, 0)))
    flat_grad = feature_grad.reshape(-1, chans)
    temporal_terms = []
    total = feature_grad.astype(jnp.float32)
    for k in range(3):
        temporal_terms.append(tdot(padded[k:k + nframes].reshape(-1, chans), flat_grad))
        back = jnp.dot(gpadded[2 - k:2 - k + nframes].reshape(-1, chans), temporal_weight[k].T, preferred_element_type=jnp.float32)
        total = total + back.reshape(inputs.shape)
    scale = 1.0 / jnp.sqrt(jnp.float32(TOKENS))
    temporal_grad = jnp.stack(temporal_terms) * scale
    spatial_grad = spatial_sum * scale
    return (total.astype(jnp.bfloat16), temporal_grad, spatial_grad)
```

```python
import functools

import jax
import jax.numpy as jnp
from jax import lax
from jax.experimental import pallas as pl
from jax.experimental.pallas import tpu as pltpu
from jax.sharding import PartitionSpec as P

MESH = pl.DeviceIdType.MESH
F32 = jnp.float32
BF16 = jnp.bfloat16
PIPES = 3
ROWS = 1024


def dot(left, right):
    return jnp.dot(left, right, preferred_element_type=F32)


def dot_t(left, right):
    return lax.dot_general(left, right, (((1,), (1,)), ((), ())), preferred_element_type=F32)


def kernel(nz, n, x_hbm, tw_hbm, sw_hbm, g_hbm, ig_hbm, tap_hbm,
           xin, gp, tw, sw, u, gext, ft3, gt, taps, part, outs,
           sb0, rb0, sb1, rb1, own1, sb2, rb2, red, rb3, agz, ag, other,
           local_sem, out_sem, tap_sem, halo_send, halo_recv, send_sem, recv_sem):
    nframes, nrows, ncols, chans = x_hbm.shape
    npairs = nframes // 2
    pix = nrows * ncols
    z = lax.axis_index("frame")
    row = lax.axis_index("row")
    nrow = 2 * n * n
    core = row % 2
    y = (row // 2) % n
    x = row // (2 * n)
    ca = x * (1 - core) + y * core
    cb = y * (1 - core) + x * core
    stride_a = 2 * n * (1 - core) + 2 * core
    stride_b = 2 * (1 - core) + 2 * n * core
    mate = (z, row + 1 - 2 * core)

    def peer_a(o):
        return (z, row + ((ca + o) % n - ca) * stride_a)

    def peer_b(o):
        return (z, row + ((cb + o) % n - cb) * stride_b)

    def peer_z(o):
        return ((z + o) % nz, row)

    down, up = (z, (row + 1) % nrow), (z, (row + nrow - 1) % nrow)
    nxt, prv = peer_z(1), peer_z(nz - 1)

    loads = [
        pltpu.make_async_copy(g_hbm, gp.at[:, pl.ds(1, nrows)], local_sem.at[0]),
        pltpu.make_async_copy(sw_hbm, sw, local_sem.at[1]),
        pltpu.make_async_copy(tw_hbm, tw, local_sem.at[2]),
        pltpu.make_async_copy(x_hbm, xin.at[pl.ds(1, nframes)], local_sem.at[3]),
    ]
    for load in loads:
        load.start()
    barrier = pltpu.get_barrier_semaphore()
    outer = (z, (row + nrow + 2 * core - 1) % nrow)
    partners = [mate, outer]
    partners += [peer_a(o) for o in range(1, n)] + [peer_b(o) for o in range(1, n)]
    partners += [peer_z(o) for o in range(1, nz)]
    for device in partners:
        pl.semaphore_signal(barrier, inc=1, device_id=device, device_id_type=MESH)
    pl.semaphore_wait(barrier, len(partners))

    def remote(src, dst, sends, recvs, slot, device):
        return pltpu.make_async_remote_copy(
            src_ref=src, dst_ref=dst, send_sem=sends.at[slot], recv_sem=recvs.at[slot],
            device_id=device, device_id_type=MESH)

    def halo(src, dst, slot, device):
        return remote(src, dst, halo_send, halo_recv, slot, device)

    rows_down = halo(g_hbm.at[:, nrows - 1], gp.at[:, 0], 0, down)
    rows_up = halo(g_hbm.at[:, 0], gp.at[:, nrows + 1], 1, up)
    x_next = halo(x_hbm.at[nframes - 1], xin.at[0], 2, nxt)
    x_prev = halo(x_hbm.at[0], xin.at[nframes + 1], 3, prv)
    for copy in (rows_down, rows_up, x_next, x_prev):
        copy.start()

    def frame(i):
        return xin[i].reshape(pix, chans)

    column = lax.broadcasted_iota(jnp.int32, (pix, chans), 0) % ncols
    lane = lax.broadcasted_iota(jnp.int32, (chans, pix), 1) % ncols

    def pair_sum(j):
        u[j] = (frame(j).astype(F32) + frame(j + 1).astype(F32)).astype(BF16)

    def features(i):
        total = dot(u[2 * i], tw[0]) + dot(u[2 * i + 1], tw[1]) + dot(u[2 * i + 2], tw[2])
        total = total + (frame(2 * i + 1).astype(F32) + frame(2 * i + 2).astype(F32))
        flip = total.T
        at = pl.ds(i * pix, pix)
        ft3[pl.ds(chans, chans), at] = flip.astype(BF16)
        right = jnp.where(lane == 0, 0.0, pltpu.roll(flip, 1, 1))
        ft3[pl.ds(0, chans), at] = right.astype(BF16)
        left = jnp.where(lane == ncols - 1, 0.0, pltpu.roll(flip, pix - 1, 1))
        ft3[pl.ds(2 * chans, chans), at] = left.astype(BF16)

    def g_rows(i, a):
        return gp[i, pl.ds(2 - a, nrows)].reshape(pix, chans)

    def feature_grad(i):
        wide = dot_t(g_rows(i, 0), sw[0]) + dot_t(g_rows(i, 1), sw[1]) + dot_t(g_rows(i, 2), sw[2])
        low, mid, high = (wide[:, b * chans:(b + 1) * chans] for b in range(3))
        low = jnp.where(column == ncols - 1, 0.0, pltpu.roll(low, pix - 1, 0))
        high = jnp.where(column == 0, 0.0, pltpu.roll(high, 1, 0))
        grad = 0.5 * (low + mid + high)
        gext[i + 1] = grad.astype(BF16)
        gt[:, pl.ds(i * pix, pix)] = grad.T.astype(BF16)

    loads[2].wait()
    loads[3].wait()
    for j in range(1, nframes):
        pair_sum(j)
    for i in range(1, npairs - 1):
        features(i)

    loads[0].wait()
    loads[1].wait()
    rows_down.wait()
    rows_up.wait()

    @pl.when(row == 0)
    def _():
        gp[:, 0] = jnp.zeros((npairs, ncols, chans), BF16)

    @pl.when(row == nrow - 1)
    def _():
        gp[:, nrows + 1] = jnp.zeros((npairs, ncols, chans), BF16)

    feature_grad(0)
    feature_grad(npairs - 1)
    grad_prev = halo(gext.at[1], gext.at[npairs + 1], 4, prv)
    grad_next = halo(gext.at[npairs], gext.at[0], 5, nxt)
    grad_prev.start()
    grad_next.start()
    for i in range(1, npairs - 1):
        feature_grad(i)

    x_next.wait()
    x_prev.wait()

    @pl.when(z == 0)
    def _():
        xin[0] = jnp.zeros((nrows, ncols, chans), BF16)

    @pl.when(z == nz - 1)
    def _():
        xin[nframes + 1] = jnp.zeros((nrows, ncols, chans), BF16)

    pair_sum(0)
    pair_sum(nframes)
    features(0)
    features(npairs - 1)

    def temporal(k):
        total = dot(gt[:, pl.ds(0, pix)], u[k])
        for i in range(1, npairs):
            total = total + dot(gt[:, pl.ds(i * pix, pix)], u[2 * i + k])
        taps[pl.ds(k * chans, chans)] = total.T

    def spatial(a):
        total = dot(ft3[:, pl.ds(0, pix)], g_rows(0, a))
        for i in range(1, npairs):
            total = total + dot(ft3[:, pl.ds(i * pix, pix)], g_rows(i, a))
        taps[pl.ds((3 + 3 * a) * chans, 3 * chans)] = total

    half = chans // 2
    size_a, size_b, size_z = ROWS // n, ROWS // n // n, ROWS // n // n // nz
    own_cols = pl.ds(pl.multiple_of(core * half, half), half)
    mate_cols = pl.ds(pl.multiple_of((1 - core) * half, half), half)
    base_a, base_b, base_z = 1, n, 2 * n - 1
    base_gz = base_z + nz - 1
    base_gb = base_gz + nz - 1
    base_ga = base_gb + n - 1
    last = base_ga + n - 1

    def chunk(index, size):
        return pl.ds(pl.multiple_of(index * size, size), size)

    def link(p, src, dst, slot, device):
        return remote(src, dst, send_sem.at[p], recv_sem.at[p], slot, device)

    def core_copy(p):
        return link(p, sb0.at[p], rb0.at[p], 0, mate)

    def a_copies(p):
        return [link(p, sb1.at[p, chunk((ca + o) % n, size_a)], rb1.at[p, o - 1], base_a + o - 1, peer_a(o))
                for o in range(1, n)]

    def b_copies(p):
        return [link(p, sb2.at[p, chunk((cb + o) % n, size_b)], rb2.at[p, o - 1], base_b + o - 1, peer_b(o))
                for o in range(1, n)]

    def z_copies(p):
        return [link(p, red.at[p, chunk((z + o) % nz, size_z)], rb3.at[p, o - 1], base_z + o - 1, peer_z(o))
                for o in range(1, nz)]

    def gz_copies(p):
        own = agz.at[p, chunk(z, size_z)]
        return [link(p, own, own, base_gz + o - 1, peer_z(o)) for o in range(1, nz)]

    def gb_copies(p):
        own = ag.at[p, chunk(ca * n + cb, size_b)]
        return [link(p, own, own, base_gb + o - 1, peer_b(o)) for o in range(1, n)]

    def ga_copies(p):
        own = ag.at[p, chunk(ca, size_a)]
        return [link(p, own, own, base_ga + o - 1, peer_a(o)) for o in range(1, n)]

    def mate_copy(p):
        return link(p, ag.at[p], other.at[p], last, mate)

    def begin(p):
        sb0[p] = taps[pl.ds(p * ROWS, ROWS), mate_cols].astype(BF16)
        core_copy(p).start()

    def step_core(p):
        core_copy(p).wait()
        total = taps[pl.ds(p * ROWS, ROWS), own_cols] + rb0[p].astype(F32)
        sb1[p] = total.astype(BF16)
        for copy in a_copies(p):
            copy.start()
        mine = pl.ds(pl.multiple_of(p * ROWS + ca * size_a, size_a), size_a)
        own1[p] = taps[mine, own_cols] + rb0[p, chunk(ca, size_a)].astype(F32)

    def step_a(p):
        for copy in a_copies(p):
            copy.wait()
        total = own1[p]
        for o in range(1, n):
            total = total + rb1[p, o - 1].astype(F32)
        own1[p] = total
        sb2[p] = total.astype(BF16)
        for copy in b_copies(p):
            copy.start()

    def step_b(p):
        for copy in b_copies(p):
            copy.wait()
        total = own1[p, chunk(cb, size_b)]
        for o in range(1, n):
            total = total + rb2[p, o - 1].astype(F32)
        red[p] = total
        for copy in z_copies(p):
            copy.start()

    def step_z(p):
        for copy in z_copies(p):
            copy.wait()
        total = red[p, chunk(z, size_z)]
        for o in range(1, nz):
            total = total + rb3[p, o - 1]
        agz[p, chunk(z, size_z)] = total
        for copy in gz_copies(p):
            copy.start()

    def step_gz(p):
        for copy in gz_copies(p):
            copy.wait()
        ag[p, chunk(ca * n + cb, size_b)] = agz[p].astype(BF16)
        for copy in gb_copies(p):
            copy.start()

    def step_gb(p):
        for copy in gb_copies(p):
            copy.wait()
        for copy in ga_copies(p):
            copy.start()

    def tap_copy(p, src, cols, slot):
        return pltpu.make_async_copy(
            src.at[p], tap_hbm.at[pl.ds(p * ROWS, ROWS), cols], tap_sem.at[2 * p + slot])

    def step_ga(p):
        for copy in ga_copies(p):
            copy.wait()
        mate_copy(p).start()
        tap_copy(p, ag, own_cols, 0).start()

    def step_mate(p):
        mate_copy(p).wait()
        tap_copy(p, other, mate_cols, 1).start()

    def out_copy(t):
        return pltpu.make_async_copy(outs.at[t], ig_hbm.at[t], out_sem.at[t])

    def put(t, value):
        outs[t] = value.astype(BF16).reshape(nrows, ncols, chans)
        out_copy(t).start()

    def input_grad(i):
        grad = gext[i + 1]
        base = grad.astype(F32) + dot_t(grad, tw[1])
        first = dot_t(grad, tw[0])
        final = dot_t(grad, tw[2])
        if i == 0:
            part[0] = base + first
        else:
            put(2 * i, base + first + part[2])
            put(2 * i - 1, part[1] + first)
        part[1] = base + final
        part[2] = final

    for k in range(3):
        temporal(k)
    spatial(0)
    begin(0)
    spatial(1)
    begin(1)
    step_core(0)
    spatial(2)
    begin(2)
    step_core(1)
    step_a(0)
    input_grad(0)
    step_core(2)
    step_b(0)
    step_a(1)
    input_grad(1)
    step_z(0)
    step_b(1)
    step_a(2)
    input_grad(2)
    step_gz(0)
    step_z(1)
    step_b(2)
    input_grad(3)
    step_gb(0)
    step_gz(1)
    step_z(2)

    grad_prev.wait()
    grad_next.wait()

    @pl.when(z == 0)
    def _():
        gext[0] = jnp.zeros((pix, chans), BF16)

    @pl.when(z == nz - 1)
    def _():
        gext[npairs + 1] = jnp.zeros((pix, chans), BF16)

    put(0, part[0] + dot_t(gext[0], tw[2]))
    put(nframes - 1, part[1] + dot_t(gext[npairs + 1], tw[0]))
    step_ga(0)
    step_gb(1)
    step_gz(2)
    step_mate(0)
    step_ga(1)
    step_gb(2)
    step_mate(1)
    step_ga(2)
    step_mate(2)
    for t in range(nframes):
        out_copy(t).wait()
    for p in range(PIPES):
        tap_copy(p, ag, own_cols, 0).wait()
        tap_copy(p, other, mate_cols, 1).wait()


def solution(mesh):
    nz = mesh.shape["frame"]
    n = 1
    while 2 * n * n < mesh.shape["row"]:
        n += 1

    def body(inputs, temporal_weight, spatial_weight, pooled_grad):
        nframes, nrows, ncols, chans = inputs.shape
        npairs = nframes // 2
        pix = nrows * ncols
        half = chans // 2
        size_a, size_b, size_z = ROWS // n, ROWS // n // n, ROWS // n // n // nz
        pixels = nframes * nz * nrows * mesh.shape["row"] * ncols
        slots = 2 * (1 + 2 * (n - 1) + nz - 1)
        any_spec = pl.BlockSpec(memory_space=pl.ANY)
        spatial = spatial_weight.reshape(3, 3 * chans, chans)
        input_grad, taps = pl.pallas_call(
            functools.partial(kernel, nz, n),
            out_shape=[
                jax.ShapeDtypeStruct(inputs.shape, BF16),
                jax.ShapeDtypeStruct((12 * chans, chans), BF16),
            ],
            in_specs=[any_spec] * 4,
            out_specs=[any_spec] * 2,
            scratch_shapes=[
                pltpu.VMEM((nframes + 2, nrows, ncols, chans), BF16),
                pltpu.VMEM((npairs, nrows + 2, ncols, chans), BF16),
                pltpu.VMEM((3, chans, chans), BF16),
                pltpu.VMEM((3, 3 * chans, chans), BF16),
                pltpu.VMEM((nframes + 1, pix, chans), BF16),
                pltpu.VMEM((npairs + 2, pix, chans), BF16),
                pltpu.VMEM((3 * chans, npairs * pix), BF16),
                pltpu.VMEM((chans, npairs * pix), BF16),
                pltpu.VMEM((12 * chans, chans), F32),
                pltpu.VMEM((3, pix, chans), F32),
                pltpu.VMEM((nframes, nrows, ncols, chans), BF16),
                pltpu.VMEM((PIPES, ROWS, half), BF16),
                pltpu.VMEM((PIPES, ROWS, half), BF16),
                pltpu.VMEM((PIPES, ROWS, half), BF16),
                pltpu.VMEM((PIPES, n - 1, size_a, half), BF16),
                pltpu.VMEM((PIPES, size_a, half), F32),
                pltpu.VMEM((PIPES, size_a, half), BF16),
                pltpu.VMEM((PIPES, n - 1, size_b, half), BF16),
                pltpu.VMEM((PIPES, size_b, half), F32),
                pltpu.VMEM((PIPES, nz - 1, size_z, half), F32),
                pltpu.VMEM((PIPES, size_b, half), F32),
                pltpu.VMEM((PIPES, ROWS, half), BF16),
                pltpu.VMEM((PIPES, ROWS, half), BF16),
                pltpu.SemaphoreType.DMA((4,)),
                pltpu.SemaphoreType.DMA((nframes,)),
                pltpu.SemaphoreType.DMA((2 * PIPES,)),
                pltpu.SemaphoreType.DMA((6,)),
                pltpu.SemaphoreType.DMA((6,)),
                pltpu.SemaphoreType.DMA((PIPES, slots)),
                pltpu.SemaphoreType.DMA((PIPES, slots)),
            ],
            compiler_params=pltpu.CompilerParams(
                collective_id=0, has_side_effects=True, vmem_limit_bytes=56 * 1024 * 1024),
            cost_estimate=pl.CostEstimate(
                flops=28 * 2 * npairs * pix * chans * chans, bytes_accessed=10 * 2**20, transcendentals=0),
            name="block",
        )(inputs, temporal_weight, spatial, pooled_grad)
        scale = 1.0 / jnp.sqrt(F32(pixels))
        temporal_grad = taps[:3 * chans].astype(F32).reshape(3, chans, chans) * scale
        spatial_grad = taps[3 * chans:].astype(F32).reshape(3, 3, chans, chans) * (0.5 * scale)
        return input_grad, temporal_grad, spatial_grad

    in_specs = (P("frame", "row", None, None), P(), P(), P("frame", "row", None, None))
    out_specs = (P("frame", "row", None, None), P(), P())
    return jax.shard_map(body, mesh=mesh, in_specs=in_specs, out_specs=out_specs, check_vma=False)
```

```python
import functools

import jax
import jax.numpy as jnp
from jax import lax
from jax.experimental import pallas as pl
from jax.experimental.pallas import tpu as pltpu
from jax.sharding import PartitionSpec as P

MESH = pl.DeviceIdType.MESH
F32 = jnp.float32
BF16 = jnp.bfloat16
PIPES = 4
BLOCK = 768


def dot(left, right):
    return jnp.dot(left, right, preferred_element_type=F32)


def dot_t(left, right):
    return lax.dot_general(left, right, (((1,), (1,)), ((), ())), preferred_element_type=F32)


def kernel(nz, n, scale, x_hbm, tw_hbm, sw_hbm, g_hbm, outs, tgrad, sgrad,
           xin, gp, tw, sw, u, gacc, gext, ft3, gt, taps, part,
           sb0, rb0, sb1, rb1, own1, zb, ag, other,
           local_sem, halo_send, halo_recv, send_sem, recv_sem):
    nframes, nrows, ncols, chans = x_hbm.shape
    npairs = nframes // 2
    pix = nrows * ncols
    z = lax.axis_index("frame")
    row = lax.axis_index("row")
    nrow = 2 * n * n
    core = row % 2
    y = (row // 2) % n
    x = row // (2 * n)
    chip = row // 2
    mate = (z, row + 1 - 2 * core)

    def plane_index(o):
        return (x + o // n) % n * n + (y + o % n) % n

    def peer_xy(o):
        return (z, 2 * plane_index(o) + core)

    def peer_z(o):
        return ((z + o) % nz, row)

    plane = sorted(range(1, n * n), key=lambda o: -min(o // n, n - o // n) - min(o % n, n - o % n))
    ring = sorted(range(1, nz), key=lambda o: -min(o, nz - o))
    down, up = (z, (row + 1) % nrow), (z, (row + nrow - 1) % nrow)
    nxt, prv = peer_z(1), peer_z(nz - 1)

    loads = [
        pltpu.make_async_copy(g_hbm, gp.at[:, pl.ds(1, nrows)], local_sem.at[0]),
        pltpu.make_async_copy(sw_hbm, sw, local_sem.at[1]),
        pltpu.make_async_copy(tw_hbm, tw, local_sem.at[2]),
        pltpu.make_async_copy(x_hbm, xin.at[pl.ds(1, nframes)], local_sem.at[3]),
    ]
    barrier = pltpu.get_barrier_semaphore()
    outer = (z, (row + nrow + 2 * core - 1) % nrow)
    partners = [mate, outer] + [peer_xy(o) for o in plane] + [peer_z(o) for o in ring]
    for device in partners:
        pl.semaphore_signal(barrier, inc=1, device_id=device, device_id_type=MESH)
    for load in loads:
        load.start()
    pl.semaphore_wait(barrier, len(partners))

    def remote(src, dst, sends, recvs, slot, device):
        return pltpu.make_async_remote_copy(
            src_ref=src, dst_ref=dst, send_sem=sends.at[slot], recv_sem=recvs.at[slot],
            device_id=device, device_id_type=MESH)

    def halo(src, dst, slot, device):
        return remote(src, dst, halo_send, halo_recv, slot, device)

    x_next = halo(x_hbm.at[nframes - 1], xin.at[0], 2, nxt)
    x_prev = halo(x_hbm.at[0], xin.at[nframes + 1], 3, prv)
    rows_down = halo(g_hbm.at[:, nrows - 1], gp.at[:, 0], 0, down)
    rows_up = halo(g_hbm.at[:, 0], gp.at[:, nrows + 1], 1, up)
    for copy in (x_next, x_prev, rows_down, rows_up):
        copy.start()

    def frame(i):
        return xin[i].reshape(pix, chans)

    lane = lax.broadcasted_iota(jnp.int32, (chans, pix), 1) % ncols

    def pair_sum(j):
        u[j] = (frame(j).astype(F32) + frame(j + 1).astype(F32)).astype(BF16)

    def features(i):
        total = dot(u[2 * i], tw[0]) + dot(u[2 * i + 1], tw[1]) + dot(u[2 * i + 2], tw[2])
        total = total + (frame(2 * i + 1).astype(F32) + frame(2 * i + 2).astype(F32))
        flip = total.T
        at = pl.ds(i * pix, pix)
        ft3[pl.ds(chans, chans), at] = flip.astype(BF16)
        right = jnp.where(lane == 0, 0.0, pltpu.roll(flip, 1, 1))
        ft3[pl.ds(0, chans), at] = right.astype(BF16)
        left = jnp.where(lane == ncols - 1, 0.0, pltpu.roll(flip, pix - 1, 1))
        ft3[pl.ds(2 * chans, chans), at] = left.astype(BF16)

    def g_rows(i, first, count):
        return gp[i, pl.ds(first, count)].reshape(count * ncols, chans)

    def shifted(wide):
        column = lax.broadcasted_iota(jnp.int32, (wide.shape[0], chans), 0) % ncols
        low, mid, high = (wide[:, b * chans:(b + 1) * chans] for b in range(3))
        low = jnp.where(column == ncols - 1, 0.0, pltpu.roll(low, wide.shape[0] - 1, 0))
        high = jnp.where(column == 0, 0.0, pltpu.roll(high, 1, 0))
        return low + mid + high

    edge = pix - ncols

    def grad_own(i):
        gacc[i] = shifted(dot_t(g_rows(i, 1, nrows), sw[1]))
        gacc[i, pl.ds(0, edge)] += shifted(dot_t(g_rows(i, 2, nrows - 1), sw[0]))
        gacc[i, pl.ds(ncols, edge)] += shifted(dot_t(g_rows(i, 1, nrows - 1), sw[2]))

    def grad_halo():
        first = shifted(dot_t(gp[:, 0].reshape(npairs * ncols, chans), sw[2]))
        final = shifted(dot_t(gp[:, nrows + 1].reshape(npairs * ncols, chans), sw[0]))
        for i in range(npairs):
            gacc[i, pl.ds(0, ncols)] += first[i * ncols:(i + 1) * ncols]
            gacc[i, pl.ds(edge, ncols)] += final[i * ncols:(i + 1) * ncols]

    def grad_done(i):
        grad = 0.5 * gacc[i]
        gext[i + 1] = grad.astype(BF16)
        gt[:, pl.ds(i * pix, pix)] = grad.T.astype(BF16)

    def outer_sum(i, left, first, count):
        return dot(ft3[:, pl.ds(i * pix + left * ncols, count * ncols)], g_rows(i, first, count))

    def spatial_own(a):
        left, first, count = ((0, 2, nrows - 1), (0, 1, nrows), (1, 1, nrows - 1))[a]
        total = outer_sum(1, left, first, count)
        for i in range(2, npairs - 1):
            total = total + outer_sum(i, left, first, count)
        taps[pl.ds(a * BLOCK, BLOCK)] = total

    def spatial_rest(a):
        total = taps[pl.ds(a * BLOCK, BLOCK)]
        for i in range(1, npairs - 1):
            if a == 0:
                total = total + outer_sum(i, nrows - 1, nrows + 1, 1)
            if a == 2:
                total = total + outer_sum(i, 0, 0, 1)
        for i in (0, npairs - 1):
            total = total + outer_sum(i, 0, 2 - a, nrows)
        taps[pl.ds(a * BLOCK, BLOCK)] = total

    def temporal():
        for k in range(3):
            total = dot(gt[:, pl.ds(0, pix)], u[k])
            for i in range(1, npairs):
                total = total + dot(gt[:, pl.ds(i * pix, pix)], u[2 * i + k])
            taps[pl.ds(3 * BLOCK + k * chans, chans)] = total.T

    half = chans // 2
    size = BLOCK // (n * n)
    own_cols = pl.ds(pl.multiple_of(core * half, half), half)
    mate_cols = pl.ds(pl.multiple_of((1 - core) * half, half), half)
    base_z = n * n
    base_g = base_z + nz - 1
    last = base_g + n * n - 1

    def chunk(index):
        return pl.ds(pl.multiple_of(index * size, size), size)

    def link(p, src, dst, slot, device):
        return remote(src, dst, send_sem.at[p], recv_sem.at[p], slot, device)

    def core_copy(p):
        return link(p, sb0.at[p], rb0.at[p], 0, mate)

    def plane_copies(p):
        return [link(p, sb1.at[p, chunk(plane_index(o))], rb1.at[p, o - 1], o, peer_xy(o)) for o in plane]

    def ring_copies(p):
        return [link(p, zb.at[p, z], zb.at[p, z], base_z + o - 1, peer_z(o)) for o in ring]

    def gather_copies(p):
        own = ag.at[p, chunk(chip)]
        return [link(p, own, own, base_g + o - 1, peer_xy(o)) for o in plane]

    def mate_copy(p):
        return link(p, ag.at[p], other.at[p], last, mate)

    def begin(p):
        sb0[p] = taps[pl.ds(p * BLOCK, BLOCK), mate_cols].astype(BF16)
        core_copy(p).start()

    def step_core(p):
        core_copy(p).wait()
        total = taps[pl.ds(p * BLOCK, BLOCK), own_cols] + rb0[p].astype(F32)
        sb1[p] = total.astype(BF16)
        for copy in plane_copies(p):
            copy.start()
        mine = pl.ds(pl.multiple_of(p * BLOCK + chip * size, size), size)
        own1[p] = taps[mine, own_cols] + rb0[p, chunk(chip)].astype(F32)

    def step_plane(p):
        for copy in plane_copies(p):
            copy.wait()
        total = own1[p]
        for o in plane:
            total = total + rb1[p, o - 1].astype(F32)
        zb[p, z] = total.astype(BF16)
        for copy in ring_copies(p):
            copy.start()

    def step_ring(p):
        for copy in ring_copies(p):
            copy.wait()
        total = zb[p, 0].astype(F32)
        for k in range(1, nz):
            total = total + zb[p, k].astype(F32)
        ag[p, chunk(chip)] = total.astype(BF16)
        for copy in gather_copies(p):
            copy.start()

    def finish(p, half_ref, cols):
        value = half_ref[p].astype(F32)
        if p < 3:
            sgrad[pl.ds(p * BLOCK, BLOCK), cols] = value * (0.5 * scale)
        else:
            tgrad[:, cols] = value * scale

    def step_gather(p):
        for copy in gather_copies(p):
            copy.wait()
        mate_copy(p).start()
        finish(p, ag, own_cols)

    def step_mate(p):
        mate_copy(p).wait()
        finish(p, other, mate_cols)

    def put(t, value):
        outs[t] = value.astype(BF16).reshape(nrows, ncols, chans)

    def input_grad(i):
        grad = gext[i + 1]
        base = grad.astype(F32) + dot_t(grad, tw[1])
        first = dot_t(grad, tw[0])
        final = dot_t(grad, tw[2])
        if i == 0:
            part[0] = base + first
        else:
            put(2 * i, base + first + part[2])
            put(2 * i - 1, part[1] + first)
        part[1] = base + final
        part[2] = final

    loads[2].wait()
    loads[3].wait()
    for j in range(1, nframes):
        pair_sum(j)
    for i in range(1, npairs - 1):
        features(i)
    loads[0].wait()
    loads[1].wait()
    for i in range(npairs):
        grad_own(i)
    for a in range(3):
        spatial_own(a)

    rows_down.wait()
    rows_up.wait()

    @pl.when(row == 0)
    def _():
        gp[:, 0] = jnp.zeros((npairs, ncols, chans), BF16)

    @pl.when(row == nrow - 1)
    def _():
        gp[:, nrows + 1] = jnp.zeros((npairs, ncols, chans), BF16)

    grad_halo()
    grad_done(0)
    grad_done(npairs - 1)
    grad_prev = halo(gext.at[1], gext.at[npairs + 1], 4, prv)
    grad_next = halo(gext.at[npairs], gext.at[0], 5, nxt)
    grad_prev.start()
    grad_next.start()
    x_next.wait()
    x_prev.wait()

    @pl.when(z == 0)
    def _():
        xin[0] = jnp.zeros((nrows, ncols, chans), BF16)

    @pl.when(z == nz - 1)
    def _():
        xin[nframes + 1] = jnp.zeros((nrows, ncols, chans), BF16)

    pair_sum(0)
    pair_sum(nframes)
    features(0)
    features(npairs - 1)
    spatial_rest(0)
    begin(0)
    spatial_rest(1)
    begin(1)
    step_core(0)
    spatial_rest(2)
    begin(2)
    step_core(1)
    for i in range(1, npairs - 1):
        grad_done(i)
    step_core(2)
    temporal()
    begin(3)
    input_grad(0)
    step_core(3)
    step_plane(0)
    input_grad(1)
    step_plane(1)
    input_grad(2)
    step_plane(2)
    input_grad(3)
    step_plane(3)
    step_ring(0)
    step_ring(1)
    step_ring(2)
    step_ring(3)

    grad_prev.wait()
    grad_next.wait()

    @pl.when(z == 0)
    def _():
        gext[0] = jnp.zeros((pix, chans), BF16)

    @pl.when(z == nz - 1)
    def _():
        gext[npairs + 1] = jnp.zeros((pix, chans), BF16)

    put(0, part[0] + dot_t(gext[0], tw[2]))
    put(nframes - 1, part[1] + dot_t(gext[npairs + 1], tw[0]))
    for p in range(PIPES):
        step_gather(p)
        if p:
            step_mate(p - 1)
    step_mate(PIPES - 1)


def write_out(grad, temporal, spatial, grad_hbm, temporal_hbm, spatial_hbm, sems):
    copies = [pltpu.make_async_copy(grad.at[t], grad_hbm.at[t], sems.at[t]) for t in range(grad.shape[0])]
    held, kept = (temporal, spatial), (temporal_hbm, spatial_hbm)
    for part in range(2):
        for k in range(held[part].shape[0]):
            copies.append(pltpu.make_async_copy(held[part].at[k], kept[part].at[k], sems.at[len(copies)]))
    for copy in copies:
        copy.start()
    for copy in copies:
        copy.wait()


def solution(mesh):
    nz = mesh.shape["frame"]
    n = 1
    while 2 * n * n < mesh.shape["row"]:
        n += 1

    def body(inputs, temporal_weight, spatial_weight, pooled_grad):
        nframes, nrows, ncols, chans = inputs.shape
        npairs = nframes // 2
        pix = nrows * ncols
        half = chans // 2
        size = BLOCK // (n * n)
        scale = float(nframes * nz * nrows * mesh.shape["row"] * ncols) ** -0.5
        slots = 2 * n * n + nz - 1
        any_spec = pl.BlockSpec(memory_space=pltpu.HBM)
        vmem_spec = pl.BlockSpec(memory_space=pltpu.VMEM)
        spatial = spatial_weight.reshape(3, 3 * chans, chans)
        input_grad, temporal_grad, spatial_grad = pl.pallas_call(
            functools.partial(kernel, nz, n, scale),
            out_shape=[
                pltpu.VMEM(inputs.shape, BF16),
                pltpu.VMEM((3 * chans, chans), F32),
                pltpu.VMEM((9 * chans, chans), F32),
            ],
            in_specs=[any_spec] * 4,
            out_specs=[vmem_spec] * 3,
            scratch_shapes=[
                pltpu.VMEM((nframes + 2, nrows, ncols, chans), BF16),
                pltpu.VMEM((npairs, nrows + 2, ncols, chans), BF16),
                pltpu.VMEM((3, chans, chans), BF16),
                pltpu.VMEM((3, 3 * chans, chans), BF16),
                pltpu.VMEM((nframes + 1, pix, chans), BF16),
                pltpu.VMEM((npairs, pix, chans), F32),
                pltpu.VMEM((npairs + 2, pix, chans), BF16),
                pltpu.VMEM((3 * chans, npairs * pix), BF16),
                pltpu.VMEM((chans, npairs * pix), BF16),
                pltpu.VMEM((12 * chans, chans), F32),
                pltpu.VMEM((3, pix, chans), F32),
                pltpu.VMEM((PIPES, BLOCK, half), BF16),
                pltpu.VMEM((PIPES, BLOCK, half), BF16),
                pltpu.VMEM((PIPES, BLOCK, half), BF16),
                pltpu.VMEM((PIPES, n * n - 1, size, half), BF16),
                pltpu.VMEM((PIPES, size, half), F32),
                pltpu.VMEM((PIPES, nz, size, half), BF16),
                pltpu.VMEM((PIPES, BLOCK, half), BF16),
                pltpu.VMEM((PIPES, BLOCK, half), BF16),
                pltpu.SemaphoreType.DMA((4,)),
                pltpu.SemaphoreType.DMA((6,)),
                pltpu.SemaphoreType.DMA((6,)),
                pltpu.SemaphoreType.DMA((PIPES, slots)),
                pltpu.SemaphoreType.DMA((PIPES, slots)),
            ],
            compiler_params=pltpu.CompilerParams(
                collective_id=0, has_side_effects=True, vmem_limit_bytes=58 * 1024 * 1024),
            cost_estimate=pl.CostEstimate(
                flops=28 * 2 * npairs * pix * chans * chans, bytes_accessed=10 * 2**20, transcendentals=0),
            name="block",
        )(inputs, temporal_weight, spatial, pooled_grad)
        input_grad, temporal_grad, spatial_grad = pl.pallas_call(
            write_out,
            out_shape=[
                jax.ShapeDtypeStruct(inputs.shape, BF16),
                jax.ShapeDtypeStruct((3, chans, chans), F32),
                jax.ShapeDtypeStruct((9, chans, chans), F32),
            ],
            in_specs=[pl.BlockSpec(memory_space=pl.ANY)] * 3,
            out_specs=[any_spec] * 3,
            scratch_shapes=[pltpu.SemaphoreType.DMA((nframes + 12,))],
            compiler_params=pltpu.CompilerParams(vmem_limit_bytes=2**20),
            name="write_out",
        )(input_grad, temporal_grad.reshape(3, chans, chans), spatial_grad.reshape(9, chans, chans))
        return input_grad, temporal_grad, spatial_grad.reshape(3, 3, chans, chans)

    in_specs = (P("frame", "row", None, None), P(), P(), P("frame", "row", None, None))
    out_specs = (P("frame", "row", None, None), P(), P())
    return jax.shard_map(body, mesh=mesh, in_specs=in_specs, out_specs=out_specs, check_vma=False)
```

```python
import functools

import jax
import jax.numpy as jnp
from jax import lax
from jax.experimental import pallas as pl
from jax.experimental.pallas import tpu as pltpu
from jax.sharding import PartitionSpec as P

MESH = pl.DeviceIdType.MESH
F32 = jnp.float32
BF16 = jnp.bfloat16
PIPES = 4
BLOCK = 768


def dot(left, right):
    return jnp.dot(left, right, preferred_element_type=F32)


def dot_t(left, right):
    return lax.dot_general(left, right, (((1,), (1,)), ((), ())), preferred_element_type=F32)


def kernel(nz, n, scale, x_hbm, tw_hbm, sw_hbm, g_hbm, outs, tgrad, sgrad,
           xin, gp, tw, sw, u, gext, ft3, gt, taps, part,
           sb0, rb0, sb1, rb1, own1, zb, ag, other,
           local_sem, halo_send, halo_recv, send_sem, recv_sem, relay):
    nframes, nrows, ncols, chans = x_hbm.shape
    npairs = nframes // 2
    pix = nrows * ncols
    z = lax.axis_index("frame")
    row = lax.axis_index("row")
    nrow = 2 * n * n
    core = row % 2
    y = (row // 2) % n
    x = row // (2 * n)
    chip = row // 2
    mate = (z, row + 1 - 2 * core)

    def plane_index(o):
        return (x + o // n) % n * n + (y + o % n) % n

    def peer_xy(o):
        return (z, 2 * plane_index(o) + core)

    def peer_z(o):
        return ((z + o) % nz, row)

    plane = sorted(range(1, n * n), key=lambda o: -min(o // n, n - o // n) - min(o % n, n - o % n))
    ring = sorted(range(1, nz), key=lambda o: -min(o, nz - o))
    down, up = (z, (row + 1) % nrow), (z, (row + nrow - 1) % nrow)
    nxt, prv = peer_z(1), peer_z(nz - 1)

    loads = [
        pltpu.make_async_copy(g_hbm, gp.at[:, pl.ds(1, nrows)], local_sem.at[0]),
        pltpu.make_async_copy(sw_hbm, sw, local_sem.at[1]),
        pltpu.make_async_copy(tw_hbm, tw, local_sem.at[2]),
        pltpu.make_async_copy(x_hbm, xin.at[pl.ds(1, nframes)], local_sem.at[3]),
    ]
    barrier = pltpu.get_barrier_semaphore()
    outer = (z, (row + nrow + 2 * core - 1) % nrow)
    around = [peer_xy(1), peer_xy(n - 1), peer_xy(n), peer_xy(n * (n - 1)), nxt, prv]
    for device in [mate, outer] + around:
        pl.semaphore_signal(barrier, inc=1, device_id=device, device_id_type=MESH)
    for load in loads:
        load.start()
    pl.semaphore_wait(barrier, 2 + len(around))

    def pass_on(k):
        for device in around:
            pl.semaphore_signal(relay.at[k], inc=1, device_id=device, device_id_type=MESH)

    def hear(k):
        pl.semaphore_wait(relay.at[k], len(around))

    def remote(src, dst, sends, recvs, slot, device):
        return pltpu.make_async_remote_copy(
            src_ref=src, dst_ref=dst, send_sem=sends.at[slot], recv_sem=recvs.at[slot],
            device_id=device, device_id_type=MESH)

    def halo(src, dst, slot, device):
        return remote(src, dst, halo_send, halo_recv, slot, device)

    x_next = halo(x_hbm.at[nframes - 1], xin.at[0], 2, nxt)
    x_prev = halo(x_hbm.at[0], xin.at[nframes + 1], 3, prv)
    rows_down = halo(g_hbm.at[:, nrows - 1], gp.at[:, 0], 0, down)
    rows_up = halo(g_hbm.at[:, 0], gp.at[:, nrows + 1], 1, up)
    for copy in (x_next, x_prev, rows_down, rows_up):
        copy.start()

    def frame(i):
        return xin[i].reshape(pix, chans)

    lane = lax.broadcasted_iota(jnp.int32, (chans, pix), 1) % ncols

    def pair_sum(j):
        u[j] = (frame(j).astype(F32) + frame(j + 1).astype(F32)).astype(BF16)

    def features(i):
        total = dot(u[2 * i], tw[0]) + dot(u[2 * i + 1], tw[1]) + dot(u[2 * i + 2], tw[2])
        total = total + (frame(2 * i + 1).astype(F32) + frame(2 * i + 2).astype(F32))
        flip = total.T
        at = pl.ds(i * pix, pix)
        ft3[pl.ds(chans, chans), at] = flip.astype(BF16)
        right = jnp.where(lane == 0, 0.0, pltpu.roll(flip, 1, 1))
        ft3[pl.ds(0, chans), at] = right.astype(BF16)
        left = jnp.where(lane == ncols - 1, 0.0, pltpu.roll(flip, pix - 1, 1))
        ft3[pl.ds(2 * chans, chans), at] = left.astype(BF16)

    def g_rows(i, first, count):
        return gp[i, pl.ds(first, count)].reshape(count * ncols, chans)

    def shifted(wide):
        column = lax.broadcasted_iota(jnp.int32, (wide.shape[0], chans), 0) % ncols
        low, mid, high = (wide[:, b * chans:(b + 1) * chans] for b in range(3))
        low = jnp.where(column == ncols - 1, 0.0, pltpu.roll(low, wide.shape[0] - 1, 0))
        high = jnp.where(column == 0, 0.0, pltpu.roll(high, 1, 0))
        return low + mid + high

    def feature_grad(i):
        wide = dot_t(g_rows(i, 2, nrows), sw[0]) + dot_t(g_rows(i, 1, nrows), sw[1])
        grad = 0.5 * shifted(wide + dot_t(g_rows(i, 0, nrows), sw[2]))
        gext[i + 1] = grad.astype(BF16)
        gt[:, pl.ds(i * pix, pix)] = grad.T.astype(BF16)

    def outer_sum(i, left, first, count):
        return dot(ft3[:, pl.ds(i * pix + left * ncols, count * ncols)], g_rows(i, first, count))

    def spatial_own(a):
        left, first, count = ((0, 2, nrows - 1), (0, 1, nrows), (1, 1, nrows - 1))[a]
        total = outer_sum(1, left, first, count)
        for i in range(2, npairs - 1):
            total = total + outer_sum(i, left, first, count)
        taps[pl.ds(a * BLOCK, BLOCK)] = total

    def spatial_rest(a):
        total = taps[pl.ds(a * BLOCK, BLOCK)]
        for i in range(1, npairs - 1):
            if a == 0:
                total = total + outer_sum(i, nrows - 1, nrows + 1, 1)
            if a == 2:
                total = total + outer_sum(i, 0, 0, 1)
        for i in (0, npairs - 1):
            total = total + outer_sum(i, 0, 2 - a, nrows)
        taps[pl.ds(a * BLOCK, BLOCK)] = total

    def temporal():
        for k in range(3):
            total = dot(gt[:, pl.ds(0, pix)], u[k])
            for i in range(1, npairs):
                total = total + dot(gt[:, pl.ds(i * pix, pix)], u[2 * i + k])
            taps[pl.ds(3 * BLOCK + k * chans, chans)] = total.T

    half = chans // 2
    size = BLOCK // (n * n)
    own_cols = pl.ds(pl.multiple_of(core * half, half), half)
    mate_cols = pl.ds(pl.multiple_of((1 - core) * half, half), half)
    base_z = n * n
    base_g = base_z + nz - 1
    last = base_g + n * n - 1

    def chunk(index):
        return pl.ds(pl.multiple_of(index * size, size), size)

    def link(p, src, dst, slot, device):
        return remote(src, dst, send_sem.at[p], recv_sem.at[p], slot, device)

    def core_copy(p):
        return link(p, sb0.at[p], rb0.at[p], 0, mate)

    def plane_copies(p):
        return [link(p, sb1.at[p, chunk(plane_index(o))], rb1.at[p, o - 1], o, peer_xy(o)) for o in plane]

    def ring_copies(p):
        return [link(p, zb.at[p, z], zb.at[p, z], base_z + o - 1, peer_z(o)) for o in ring]

    def gather_copies(p):
        own = ag.at[p, chunk(chip)]
        return [link(p, own, own, base_g + o - 1, peer_xy(o)) for o in plane]

    def mate_copy(p):
        return link(p, ag.at[p], other.at[p], last, mate)

    def begin(p):
        sb0[p] = taps[pl.ds(p * BLOCK, BLOCK), mate_cols].astype(BF16)
        core_copy(p).start()

    def step_core(p):
        core_copy(p).wait()
        total = taps[pl.ds(p * BLOCK, BLOCK), own_cols] + rb0[p].astype(F32)
        sb1[p] = total.astype(BF16)
        for copy in plane_copies(p):
            copy.start()
        mine = pl.ds(pl.multiple_of(p * BLOCK + chip * size, size), size)
        own1[p] = taps[mine, own_cols] + rb0[p, chunk(chip)].astype(F32)

    def step_plane(p):
        for copy in plane_copies(p):
            copy.wait()
        total = own1[p]
        for o in plane:
            total = total + rb1[p, o - 1].astype(F32)
        zb[p, z] = total.astype(BF16)
        for copy in ring_copies(p):
            copy.start()

    def step_ring(p):
        for copy in ring_copies(p):
            copy.wait()
        total = zb[p, 0].astype(F32)
        for k in range(1, nz):
            total = total + zb[p, k].astype(F32)
        ag[p, chunk(chip)] = total.astype(BF16)
        for copy in gather_copies(p):
            copy.start()

    def finish(p, half_ref, cols):
        value = half_ref[p].astype(F32)
        if p < 3:
            sgrad[pl.ds(p * BLOCK, BLOCK), cols] = value * (0.5 * scale)
        else:
            tgrad[:, cols] = value * scale

    def step_gather(p):
        for copy in gather_copies(p):
            copy.wait()
        mate_copy(p).start()
        finish(p, ag, own_cols)

    def step_mate(p):
        mate_copy(p).wait()
        finish(p, other, mate_cols)

    def put(t, value):
        outs[t] = value.astype(BF16).reshape(nrows, ncols, chans)

    def input_grad(i):
        grad = gext[i + 1]
        base = grad.astype(F32) + dot_t(grad, tw[1])
        first = dot_t(grad, tw[0])
        final = dot_t(grad, tw[2])
        if i == 0:
            part[0] = base + first
        else:
            put(2 * i, base + first + part[2])
            put(2 * i - 1, part[1] + first)
        part[1] = base + final
        part[2] = final

    pass_on(0)
    loads[2].wait()
    loads[3].wait()
    for j in range(1, nframes):
        pair_sum(j)
    hear(0)
    pass_on(1)
    for i in range(1, npairs - 1):
        features(i)
    loads[0].wait()
    loads[1].wait()
    spatial_own(0)
    hear(1)
    pass_on(2)
    spatial_own(1)
    spatial_own(2)

    rows_down.wait()
    rows_up.wait()

    @pl.when(row == 0)
    def _():
        gp[:, 0] = jnp.zeros((npairs, ncols, chans), BF16)

    @pl.when(row == nrow - 1)
    def _():
        gp[:, nrows + 1] = jnp.zeros((npairs, ncols, chans), BF16)

    x_next.wait()
    x_prev.wait()

    @pl.when(z == 0)
    def _():
        xin[0] = jnp.zeros((nrows, ncols, chans), BF16)

    @pl.when(z == nz - 1)
    def _():
        xin[nframes + 1] = jnp.zeros((nrows, ncols, chans), BF16)

    pair_sum(0)
    pair_sum(nframes)
    features(0)
    features(npairs - 1)

    spatial_rest(0)
    begin(0)
    feature_grad(0)
    hear(2)
    step_core(0)
    spatial_rest(1)
    begin(1)
    feature_grad(npairs - 1)
    grad_prev = halo(gext.at[1], gext.at[npairs + 1], 4, prv)
    grad_next = halo(gext.at[npairs], gext.at[0], 5, nxt)
    grad_prev.start()
    grad_next.start()
    step_core(1)
    spatial_rest(2)
    begin(2)
    for i in range(1, npairs - 1):
        feature_grad(i)
    step_core(2)
    temporal()
    begin(3)
    input_grad(0)
    input_grad(1)
    step_core(3)
    input_grad(2)
    input_grad(3)
    step_plane(0)
    step_plane(1)
    step_plane(2)
    step_plane(3)
    step_ring(0)
    step_ring(1)
    step_ring(2)
    step_ring(3)

    grad_prev.wait()
    grad_next.wait()

    @pl.when(z == 0)
    def _():
        gext[0] = jnp.zeros((pix, chans), BF16)

    @pl.when(z == nz - 1)
    def _():
        gext[npairs + 1] = jnp.zeros((pix, chans), BF16)

    put(0, part[0] + dot_t(gext[0], tw[2]))
    put(nframes - 1, part[1] + dot_t(gext[npairs + 1], tw[0]))
    for p in range(PIPES):
        step_gather(p)
        if p:
            step_mate(p - 1)
    step_mate(PIPES - 1)


def write_out(grad, temporal, spatial, grad_hbm, temporal_hbm, spatial_hbm, sems):
    copies = [pltpu.make_async_copy(grad.at[t], grad_hbm.at[t], sems.at[t]) for t in range(grad.shape[0])]
    held, kept = (temporal, spatial), (temporal_hbm, spatial_hbm)
    for part in range(2):
        for k in range(held[part].shape[0]):
            copies.append(pltpu.make_async_copy(held[part].at[k], kept[part].at[k], sems.at[len(copies)]))
    for copy in copies:
        copy.start()
    for copy in copies:
        copy.wait()


def solution(mesh):
    nz = mesh.shape["frame"]
    n = 1
    while 2 * n * n < mesh.shape["row"]:
        n += 1

    def body(inputs, temporal_weight, spatial_weight, pooled_grad):
        nframes, nrows, ncols, chans = inputs.shape
        npairs = nframes // 2
        pix = nrows * ncols
        half = chans // 2
        size = BLOCK // (n * n)
        scale = float(nframes * nz * nrows * mesh.shape["row"] * ncols) ** -0.5
        slots = 2 * n * n + nz - 1
        any_spec = pl.BlockSpec(memory_space=pltpu.HBM)
        vmem_spec = pl.BlockSpec(memory_space=pltpu.VMEM)
        spatial = spatial_weight.reshape(3, 3 * chans, chans)
        input_grad, temporal_grad, spatial_grad = pl.pallas_call(
            functools.partial(kernel, nz, n, scale),
            out_shape=[
                pltpu.VMEM(inputs.shape, BF16),
                pltpu.VMEM((3 * chans, chans), F32),
                pltpu.VMEM((9 * chans, chans), F32),
            ],
            in_specs=[any_spec] * 4,
            out_specs=[vmem_spec] * 3,
            scratch_shapes=[
                pltpu.VMEM((nframes + 2, nrows, ncols, chans), BF16),
                pltpu.VMEM((npairs, nrows + 2, ncols, chans), BF16),
                pltpu.VMEM((3, chans, chans), BF16),
                pltpu.VMEM((3, 3 * chans, chans), BF16),
                pltpu.VMEM((nframes + 1, pix, chans), BF16),
                pltpu.VMEM((npairs + 2, pix, chans), BF16),
                pltpu.VMEM((3 * chans, npairs * pix), BF16),
                pltpu.VMEM((chans, npairs * pix), BF16),
                pltpu.VMEM((12 * chans, chans), F32),
                pltpu.VMEM((3, pix, chans), F32),
                pltpu.VMEM((PIPES, BLOCK, half), BF16),
                pltpu.VMEM((PIPES, BLOCK, half), BF16),
                pltpu.VMEM((PIPES, BLOCK, half), BF16),
                pltpu.VMEM((PIPES, n * n - 1, size, half), BF16),
                pltpu.VMEM((PIPES, size, half), F32),
                pltpu.VMEM((PIPES, nz, size, half), BF16),
                pltpu.VMEM((PIPES, BLOCK, half), BF16),
                pltpu.VMEM((PIPES, BLOCK, half), BF16),
                pltpu.SemaphoreType.DMA((4,)),
                pltpu.SemaphoreType.DMA((6,)),
                pltpu.SemaphoreType.DMA((6,)),
                pltpu.SemaphoreType.DMA((PIPES, slots)),
                pltpu.SemaphoreType.DMA((PIPES, slots)),
                pltpu.SemaphoreType.REGULAR((3,)),
            ],
            compiler_params=pltpu.CompilerParams(
                collective_id=0, has_side_effects=True, vmem_limit_bytes=58 * 1024 * 1024),
            cost_estimate=pl.CostEstimate(
                flops=28 * 2 * npairs * pix * chans * chans, bytes_accessed=10 * 2**20, transcendentals=0),
            name="block",
        )(inputs, temporal_weight, spatial, pooled_grad)
        input_grad, temporal_grad, spatial_grad = pl.pallas_call(
            write_out,
            out_shape=[
                jax.ShapeDtypeStruct(inputs.shape, BF16),
                jax.ShapeDtypeStruct((3, chans, chans), F32),
                jax.ShapeDtypeStruct((9, chans, chans), F32),
            ],
            in_specs=[pl.BlockSpec(memory_space=pl.ANY)] * 3,
            out_specs=[any_spec] * 3,
            scratch_shapes=[pltpu.SemaphoreType.DMA((nframes + 12,))],
            compiler_params=pltpu.CompilerParams(vmem_limit_bytes=2**20),
            name="write_out",
        )(input_grad, temporal_grad.reshape(3, chans, chans), spatial_grad.reshape(9, chans, chans))
        return input_grad, temporal_grad, spatial_grad.reshape(3, 3, chans, chans)

    in_specs = (P("frame", "row", None, None), P(), P(), P("frame", "row", None, None))
    out_specs = (P("frame", "row", None, None), P(), P())
    return jax.shard_map(body, mesh=mesh, in_specs=in_specs, out_specs=out_specs, check_vma=False)
```

```python
import functools

import jax
import jax.numpy as jnp
from jax import lax
from jax.experimental import pallas as pl
from jax.experimental.pallas import tpu as pltpu
from jax.sharding import PartitionSpec as P

MESH = pl.DeviceIdType.MESH
F32 = jnp.float32
BF16 = jnp.bfloat16
PIPES = 4
BLOCK = 768


def dot(left, right):
    return jnp.dot(left, right, preferred_element_type=F32)


def dot_t(left, right):
    return lax.dot_general(left, right, (((1,), (1,)), ((), ())), preferred_element_type=F32)


def kernel(nz, n, scale, x_hbm, tw_hbm, sw_hbm, g_hbm, outs, tgrad, sgrad,
           xin, gp, tw, sw, u, gacc, gext, ft3, gt, taps, part,
           sb0, rb0, sb1, rb1, own1, zb, ag, other,
           local_sem, halo_send, halo_recv, send_sem, recv_sem, relay):
    nframes, nrows, ncols, chans = x_hbm.shape
    npairs = nframes // 2
    pix = nrows * ncols
    z = lax.axis_index("frame")
    row = lax.axis_index("row")
    nrow = 2 * n * n
    core = row % 2
    y = (row // 2) % n
    x = row // (2 * n)
    chip = row // 2
    mate = (z, row + 1 - 2 * core)

    def plane_index(o):
        return (x + o // n) % n * n + (y + o % n) % n

    def peer_xy(o):
        return (z, 2 * plane_index(o) + core)

    def peer_z(o):
        return ((z + o) % nz, row)

    plane = sorted(range(1, n * n), key=lambda o: -min(o // n, n - o // n) - min(o % n, n - o % n))
    ring = sorted(range(1, nz), key=lambda o: -min(o, nz - o))
    down, up = (z, (row + 1) % nrow), (z, (row + nrow - 1) % nrow)
    nxt, prv = peer_z(1), peer_z(nz - 1)

    loads = [
        pltpu.make_async_copy(g_hbm, gp.at[:, pl.ds(1, nrows)], local_sem.at[0]),
        pltpu.make_async_copy(sw_hbm, sw, local_sem.at[1]),
        pltpu.make_async_copy(tw_hbm, tw, local_sem.at[2]),
        pltpu.make_async_copy(x_hbm, xin.at[pl.ds(1, nframes)], local_sem.at[3]),
    ]
    barrier = pltpu.get_barrier_semaphore()
    outer = (z, (row + nrow + 2 * core - 1) % nrow)
    around = [peer_xy(1), peer_xy(n - 1), peer_xy(n), peer_xy(n * (n - 1)), nxt, prv]
    for device in [mate, outer] + around:
        pl.semaphore_signal(barrier, inc=1, device_id=device, device_id_type=MESH)
    for load in loads:
        load.start()
    pl.semaphore_wait(barrier, 2 + len(around))

    def pass_on(k):
        for device in around:
            pl.semaphore_signal(relay.at[k], inc=1, device_id=device, device_id_type=MESH)

    def hear(k):
        pl.semaphore_wait(relay.at[k], len(around))

    def remote(src, dst, sends, recvs, slot, device):
        return pltpu.make_async_remote_copy(
            src_ref=src, dst_ref=dst, send_sem=sends.at[slot], recv_sem=recvs.at[slot],
            device_id=device, device_id_type=MESH)

    def halo(src, dst, slot, device):
        return remote(src, dst, halo_send, halo_recv, slot, device)

    x_next = halo(x_hbm.at[nframes - 1], xin.at[0], 2, nxt)
    x_prev = halo(x_hbm.at[0], xin.at[nframes + 1], 3, prv)
    rows_down = halo(g_hbm.at[:, nrows - 1], gp.at[:, 0], 0, down)
    rows_up = halo(g_hbm.at[:, 0], gp.at[:, nrows + 1], 1, up)
    for copy in (x_next, x_prev, rows_down, rows_up):
        copy.start()

    def frame(i):
        return xin[i].reshape(pix, chans)

    lane = lax.broadcasted_iota(jnp.int32, (chans, pix), 1) % ncols

    def pair_sum(j):
        u[j] = (frame(j).astype(F32) + frame(j + 1).astype(F32)).astype(BF16)

    def features(i):
        total = dot(u[2 * i], tw[0]) + dot(u[2 * i + 1], tw[1]) + dot(u[2 * i + 2], tw[2])
        total = total + (frame(2 * i + 1).astype(F32) + frame(2 * i + 2).astype(F32))
        flip = total.T
        at = pl.ds(i * pix, pix)
        ft3[pl.ds(chans, chans), at] = flip.astype(BF16)
        right = jnp.where(lane == 0, 0.0, pltpu.roll(flip, 1, 1))
        ft3[pl.ds(0, chans), at] = right.astype(BF16)
        left = jnp.where(lane == ncols - 1, 0.0, pltpu.roll(flip, pix - 1, 1))
        ft3[pl.ds(2 * chans, chans), at] = left.astype(BF16)

    def g_rows(i, first, count):
        return gp[i, pl.ds(first, count)].reshape(count * ncols, chans)

    def shifted(wide):
        column = lax.broadcasted_iota(jnp.int32, (wide.shape[0], chans), 0) % ncols
        low, mid, high = (wide[:, b * chans:(b + 1) * chans] for b in range(3))
        low = jnp.where(column == ncols - 1, 0.0, pltpu.roll(low, wide.shape[0] - 1, 0))
        high = jnp.where(column == 0, 0.0, pltpu.roll(high, 1, 0))
        return low + mid + high

    edge = pix - ncols

    def grad_own(i):
        gacc[i] = shifted(dot_t(g_rows(i, 1, nrows), sw[1]))
        gacc[i, pl.ds(0, edge)] += shifted(dot_t(g_rows(i, 2, nrows - 1), sw[0]))
        gacc[i, pl.ds(ncols, edge)] += shifted(dot_t(g_rows(i, 1, nrows - 1), sw[2]))

    def grad_halo():
        first = shifted(dot_t(gp[:, 0].reshape(npairs * ncols, chans), sw[2]))
        final = shifted(dot_t(gp[:, nrows + 1].reshape(npairs * ncols, chans), sw[0]))
        for i in range(npairs):
            gacc[i, pl.ds(0, ncols)] += first[i * ncols:(i + 1) * ncols]
            gacc[i, pl.ds(edge, ncols)] += final[i * ncols:(i + 1) * ncols]

    def grad_done(i):
        grad = 0.5 * gacc[i]
        gext[i + 1] = grad.astype(BF16)
        gt[:, pl.ds(i * pix, pix)] = grad.T.astype(BF16)

    def outer_sum(i, left, first, count):
        return dot(ft3[:, pl.ds(i * pix + left * ncols, count * ncols)], g_rows(i, first, count))

    def spatial_own(a):
        left, first, count = ((0, 2, nrows - 1), (0, 1, nrows), (1, 1, nrows - 1))[a]
        total = outer_sum(1, left, first, count)
        for i in range(2, npairs - 1):
            total = total + outer_sum(i, left, first, count)
        taps[pl.ds(a * BLOCK, BLOCK)] = total

    def spatial_rest(a):
        total = taps[pl.ds(a * BLOCK, BLOCK)]
        for i in range(1, npairs - 1):
            if a == 0:
                total = total + outer_sum(i, nrows - 1, nrows + 1, 1)
            if a == 2:
                total = total + outer_sum(i, 0, 0, 1)
        for i in (0, npairs - 1):
            total = total + outer_sum(i, 0, 2 - a, nrows)
        taps[pl.ds(a * BLOCK, BLOCK)] = total

    def temporal():
        for k in range(3):
            total = dot(gt[:, pl.ds(0, pix)], u[k])
            for i in range(1, npairs):
                total = total + dot(gt[:, pl.ds(i * pix, pix)], u[2 * i + k])
            taps[pl.ds(3 * BLOCK + k * chans, chans)] = total.T

    half = chans // 2
    size = BLOCK // (n * n)
    own_cols = pl.ds(pl.multiple_of(core * half, half), half)
    mate_cols = pl.ds(pl.multiple_of((1 - core) * half, half), half)
    base_z = n * n
    base_g = base_z + nz - 1
    last = base_g + n * n - 1

    def chunk(index):
        return pl.ds(pl.multiple_of(index * size, size), size)

    def link(p, src, dst, slot, device):
        return remote(src, dst, send_sem.at[p], recv_sem.at[p], slot, device)

    def core_copy(p):
        return link(p, sb0.at[p], rb0.at[p], 0, mate)

    def plane_copies(p):
        return [link(p, sb1.at[p, chunk(plane_index(o))], rb1.at[p, o - 1], o, peer_xy(o)) for o in plane]

    def ring_copies(p):
        return [link(p, zb.at[p, z], zb.at[p, z], base_z + o - 1, peer_z(o)) for o in ring]

    def gather_copies(p):
        own = ag.at[p, chunk(chip)]
        return [link(p, own, own, base_g + o - 1, peer_xy(o)) for o in plane]

    def mate_copy(p):
        return link(p, ag.at[p], other.at[p], last, mate)

    def begin(p):
        sb0[p] = taps[pl.ds(p * BLOCK, BLOCK), mate_cols].astype(BF16)
        core_copy(p).start()

    def step_core(p):
        core_copy(p).wait()
        total = taps[pl.ds(p * BLOCK, BLOCK), own_cols] + rb0[p].astype(F32)
        sb1[p] = total.astype(BF16)
        for copy in plane_copies(p):
            copy.start()
        mine = pl.ds(pl.multiple_of(p * BLOCK + chip * size, size), size)
        own1[p] = taps[mine, own_cols] + rb0[p, chunk(chip)].astype(F32)

    def step_plane(p):
        for copy in plane_copies(p):
            copy.wait()
        total = own1[p]
        for o in plane:
            total = total + rb1[p, o - 1].astype(F32)
        zb[p, z] = total.astype(BF16)
        for copy in ring_copies(p):
            copy.start()

    def step_ring(p):
        for copy in ring_copies(p):
            copy.wait()
        total = zb[p, 0].astype(F32)
        for k in range(1, nz):
            total = total + zb[p, k].astype(F32)
        ag[p, chunk(chip)] = total.astype(BF16)
        for copy in gather_copies(p):
            copy.start()

    def finish(p, half_ref, cols):
        value = half_ref[p].astype(F32)
        if p < 3:
            sgrad[pl.ds(p * BLOCK, BLOCK), cols] = value * (0.5 * scale)
        else:
            tgrad[:, cols] = value * scale

    def step_gather(p):
        for copy in gather_copies(p):
            copy.wait()
        mate_copy(p).start()
        finish(p, ag, own_cols)

    def step_mate(p):
        mate_copy(p).wait()
        finish(p, other, mate_cols)

    def put(t, value):
        outs[t] = value.astype(BF16).reshape(nrows, ncols, chans)

    def input_grad(i):
        grad = gext[i + 1]
        base = grad.astype(F32) + dot_t(grad, tw[1])
        first = dot_t(grad, tw[0])
        final = dot_t(grad, tw[2])
        if i == 0:
            part[0] = base + first
        else:
            put(2 * i, base + first + part[2])
            put(2 * i - 1, part[1] + first)
        part[1] = base + final
        part[2] = final

    pass_on(0)
    loads[2].wait()
    loads[3].wait()
    for j in range(1, nframes):
        pair_sum(j)
    hear(0)
    pass_on(1)
    for i in range(1, npairs - 1):
        features(i)
    loads[0].wait()
    loads[1].wait()
    grad_own(0)
    hear(1)
    pass_on(2)
    for i in range(1, npairs):
        grad_own(i)
    for a in range(3):
        spatial_own(a)
    hear(2)

    rows_down.wait()
    rows_up.wait()

    @pl.when(row == 0)
    def _():
        gp[:, 0] = jnp.zeros((npairs, ncols, chans), BF16)

    @pl.when(row == nrow - 1)
    def _():
        gp[:, nrows + 1] = jnp.zeros((npairs, ncols, chans), BF16)

    grad_halo()
    grad_done(0)
    grad_done(npairs - 1)
    grad_prev = halo(gext.at[1], gext.at[npairs + 1], 4, prv)
    grad_next = halo(gext.at[npairs], gext.at[0], 5, nxt)
    grad_prev.start()
    grad_next.start()
    x_next.wait()
    x_prev.wait()

    @pl.when(z == 0)
    def _():
        xin[0] = jnp.zeros((nrows, ncols, chans), BF16)

    @pl.when(z == nz - 1)
    def _():
        xin[nframes + 1] = jnp.zeros((nrows, ncols, chans), BF16)

    pair_sum(0)
    pair_sum(nframes)
    features(0)
    features(npairs - 1)
    spatial_rest(0)
    begin(0)
    spatial_rest(1)
    begin(1)
    step_core(0)
    spatial_rest(2)
    begin(2)
    step_core(1)
    for i in range(1, npairs - 1):
        grad_done(i)
    step_core(2)
    temporal()
    begin(3)
    input_grad(0)
    step_core(3)
    step_plane(0)
    input_grad(1)
    step_plane(1)
    input_grad(2)
    step_plane(2)
    input_grad(3)
    step_plane(3)
    step_ring(0)
    step_ring(1)
    step_ring(2)
    step_ring(3)

    grad_prev.wait()
    grad_next.wait()

    @pl.when(z == 0)
    def _():
        gext[0] = jnp.zeros((pix, chans), BF16)

    @pl.when(z == nz - 1)
    def _():
        gext[npairs + 1] = jnp.zeros((pix, chans), BF16)

    put(0, part[0] + dot_t(gext[0], tw[2]))
    put(nframes - 1, part[1] + dot_t(gext[npairs + 1], tw[0]))
    for p in range(PIPES):
        step_gather(p)
        if p:
            step_mate(p - 1)
    step_mate(PIPES - 1)


def write_out(grad, temporal, spatial, grad_hbm, temporal_hbm, spatial_hbm, sems):
    copies = [pltpu.make_async_copy(grad.at[t], grad_hbm.at[t], sems.at[t]) for t in range(grad.shape[0])]
    held, kept = (temporal, spatial), (temporal_hbm, spatial_hbm)
    for part in range(2):
        for k in range(held[part].shape[0]):
            copies.append(pltpu.make_async_copy(held[part].at[k], kept[part].at[k], sems.at[len(copies)]))
    for copy in copies:
        copy.start()
    for copy in copies:
        copy.wait()


def solution(mesh):
    nz = mesh.shape["frame"]
    n = 1
    while 2 * n * n < mesh.shape["row"]:
        n += 1

    def body(inputs, temporal_weight, spatial_weight, pooled_grad):
        nframes, nrows, ncols, chans = inputs.shape
        npairs = nframes // 2
        pix = nrows * ncols
        half = chans // 2
        size = BLOCK // (n * n)
        scale = float(nframes * nz * nrows * mesh.shape["row"] * ncols) ** -0.5
        slots = 2 * n * n + nz - 1
        any_spec = pl.BlockSpec(memory_space=pltpu.HBM)
        vmem_spec = pl.BlockSpec(memory_space=pltpu.VMEM)
        spatial = spatial_weight.reshape(3, 3 * chans, chans)
        input_grad, temporal_grad, spatial_grad = pl.pallas_call(
            functools.partial(kernel, nz, n, scale),
            out_shape=[
                pltpu.VMEM(inputs.shape, BF16),
                pltpu.VMEM((3 * chans, chans), F32),
                pltpu.VMEM((9 * chans, chans), F32),
            ],
            in_specs=[any_spec] * 4,
            out_specs=[vmem_spec] * 3,
            scratch_shapes=[
                pltpu.VMEM((nframes + 2, nrows, ncols, chans), BF16),
                pltpu.VMEM((npairs, nrows + 2, ncols, chans), BF16),
                pltpu.VMEM((3, chans, chans), BF16),
                pltpu.VMEM((3, 3 * chans, chans), BF16),
                pltpu.VMEM((nframes + 1, pix, chans), BF16),
                pltpu.VMEM((npairs, pix, chans), F32),
                pltpu.VMEM((npairs + 2, pix, chans), BF16),
                pltpu.VMEM((3 * chans, npairs * pix), BF16),
                pltpu.VMEM((chans, npairs * pix), BF16),
                pltpu.VMEM((12 * chans, chans), F32),
                pltpu.VMEM((3, pix, chans), F32),
                pltpu.VMEM((PIPES, BLOCK, half), BF16),
                pltpu.VMEM((PIPES, BLOCK, half), BF16),
                pltpu.VMEM((PIPES, BLOCK, half), BF16),
                pltpu.VMEM((PIPES, n * n - 1, size, half), BF16),
                pltpu.VMEM((PIPES, size, half), F32),
                pltpu.VMEM((PIPES, nz, size, half), BF16),
                pltpu.VMEM((PIPES, BLOCK, half), BF16),
                pltpu.VMEM((PIPES, BLOCK, half), BF16),
                pltpu.SemaphoreType.DMA((4,)),
                pltpu.SemaphoreType.DMA((6,)),
                pltpu.SemaphoreType.DMA((6,)),
                pltpu.SemaphoreType.DMA((PIPES, slots)),
                pltpu.SemaphoreType.DMA((PIPES, slots)),
                pltpu.SemaphoreType.REGULAR((3,)),
            ],
            compiler_params=pltpu.CompilerParams(
                collective_id=0, has_side_effects=True, vmem_limit_bytes=58 * 1024 * 1024),
            cost_estimate=pl.CostEstimate(
                flops=28 * 2 * npairs * pix * chans * chans, bytes_accessed=10 * 2**20, transcendentals=0),
            name="block",
        )(inputs, temporal_weight, spatial, pooled_grad)
        input_grad, temporal_grad, spatial_grad = pl.pallas_call(
            write_out,
            out_shape=[
                jax.ShapeDtypeStruct(inputs.shape, BF16),
                jax.ShapeDtypeStruct((3, chans, chans), F32),
                jax.ShapeDtypeStruct((9, chans, chans), F32),
            ],
            in_specs=[pl.BlockSpec(memory_space=pl.ANY)] * 3,
            out_specs=[any_spec] * 3,
            scratch_shapes=[pltpu.SemaphoreType.DMA((nframes + 12,))],
            compiler_params=pltpu.CompilerParams(vmem_limit_bytes=2**20),
            name="write_out",
        )(input_grad, temporal_grad.reshape(3, chans, chans), spatial_grad.reshape(9, chans, chans))
        return input_grad, temporal_grad, spatial_grad.reshape(3, 3, chans, chans)

    in_specs = (P("frame", "row", None, None), P(), P(), P("frame", "row", None, None))
    out_specs = (P("frame", "row", None, None), P(), P())
    return jax.shard_map(body, mesh=mesh, in_specs=in_specs, out_specs=out_specs, check_vma=False)
```

```python
import functools

import jax
import jax.numpy as jnp
from jax import lax
from jax.experimental import pallas as pl
from jax.experimental.pallas import tpu as pltpu
from jax.sharding import PartitionSpec as P

MESH = pl.DeviceIdType.MESH
F32 = jnp.float32
BF16 = jnp.bfloat16
PIPES = 4
BLOCK = 768


def dot(left, right):
    return jnp.dot(left, right, preferred_element_type=F32)


def dot_t(left, right):
    return lax.dot_general(left, right, (((1,), (1,)), ((), ())), preferred_element_type=F32)


def kernel(nz, n, scale, x_hbm, tw_hbm, sw_hbm, g_hbm, outs, tgrad, sgrad,
           xin, gp, tw, sw, u, gacc, gext, ft3, gt, taps, part,
           sb0, rb0, sb1, rb1, own1, zb, ag, other,
           local_sem, halo_send, halo_recv, send_sem, recv_sem, relay):
    nframes, nrows, ncols, chans = x_hbm.shape
    npairs = nframes // 2
    pix = nrows * ncols
    z = lax.axis_index("frame")
    row = lax.axis_index("row")
    nrow = 2 * n * n
    core = row % 2
    y = (row // 2) % n
    x = row // (2 * n)
    chip = row // 2
    mate = (z, row + 1 - 2 * core)

    def plane_index(o):
        return (x + o // n) % n * n + (y + o % n) % n

    def peer_xy(o):
        return (z, 2 * plane_index(o) + core)

    def peer_z(o):
        return ((z + o) % nz, row)

    plane = sorted(range(1, n * n), key=lambda o: -min(o // n, n - o // n) - min(o % n, n - o % n))
    ring = sorted(range(1, nz), key=lambda o: -min(o, nz - o))
    down, up = (z, (row + 1) % nrow), (z, (row + nrow - 1) % nrow)
    nxt, prv = peer_z(1), peer_z(nz - 1)

    loads = [
        pltpu.make_async_copy(g_hbm, gp.at[:, pl.ds(1, nrows)], local_sem.at[0]),
        pltpu.make_async_copy(sw_hbm, sw, local_sem.at[1]),
        pltpu.make_async_copy(tw_hbm, tw, local_sem.at[2]),
        pltpu.make_async_copy(x_hbm, xin.at[pl.ds(1, nframes)], local_sem.at[3]),
    ]
    barrier = pltpu.get_barrier_semaphore()
    outer = (z, (row + nrow + 2 * core - 1) % nrow)
    around = [peer_xy(1), peer_xy(n - 1), peer_xy(n), peer_xy(n * (n - 1)), nxt, prv]
    for device in [mate, outer] + around:
        pl.semaphore_signal(barrier, inc=1, device_id=device, device_id_type=MESH)
    for load in loads:
        load.start()
    pl.semaphore_wait(barrier, 2 + len(around))

    def pass_on(k):
        for device in around:
            pl.semaphore_signal(relay.at[k], inc=1, device_id=device, device_id_type=MESH)

    def hear(k):
        pl.semaphore_wait(relay.at[k], len(around))

    def remote(src, dst, sends, recvs, slot, device):
        return pltpu.make_async_remote_copy(
            src_ref=src, dst_ref=dst, send_sem=sends.at[slot], recv_sem=recvs.at[slot],
            device_id=device, device_id_type=MESH)

    def halo(src, dst, slot, device):
        return remote(src, dst, halo_send, halo_recv, slot, device)

    x_next = halo(x_hbm.at[nframes - 1], xin.at[0], 2, nxt)
    x_prev = halo(x_hbm.at[0], xin.at[nframes + 1], 3, prv)
    rows_down = halo(g_hbm.at[:, nrows - 1], gp.at[:, 0], 0, down)
    rows_up = halo(g_hbm.at[:, 0], gp.at[:, nrows + 1], 1, up)
    for copy in (x_next, x_prev, rows_down, rows_up):
        copy.start()

    def frame(i):
        return xin[i].reshape(pix, chans)

    lane = lax.broadcasted_iota(jnp.int32, (chans, pix), 1) % ncols

    def pair_sum(j):
        u[j] = (frame(j).astype(F32) + frame(j + 1).astype(F32)).astype(BF16)

    def features(i):
        total = dot(u[2 * i], tw[0]) + dot(u[2 * i + 1], tw[1]) + dot(u[2 * i + 2], tw[2])
        total = total + (frame(2 * i + 1).astype(F32) + frame(2 * i + 2).astype(F32))
        flip = total.T
        at = pl.ds(i * pix, pix)
        ft3[pl.ds(chans, chans), at] = flip.astype(BF16)
        right = jnp.where(lane == 0, 0.0, pltpu.roll(flip, 1, 1))
        ft3[pl.ds(0, chans), at] = right.astype(BF16)
        left = jnp.where(lane == ncols - 1, 0.0, pltpu.roll(flip, pix - 1, 1))
        ft3[pl.ds(2 * chans, chans), at] = left.astype(BF16)

    def g_rows(i, first, count):
        return gp[i, pl.ds(first, count)].reshape(count * ncols, chans)

    def shifted(wide):
        column = lax.broadcasted_iota(jnp.int32, (wide.shape[0], chans), 0) % ncols
        low, mid, high = (wide[:, b * chans:(b + 1) * chans] for b in range(3))
        low = jnp.where(column == ncols - 1, 0.0, pltpu.roll(low, wide.shape[0] - 1, 0))
        high = jnp.where(column == 0, 0.0, pltpu.roll(high, 1, 0))
        return low + mid + high

    edge = pix - ncols

    def grad_own(i):
        gacc[i] = shifted(dot_t(g_rows(i, 1, nrows), sw[1]))
        gacc[i, pl.ds(0, edge)] += shifted(dot_t(g_rows(i, 2, nrows - 1), sw[0]))
        gacc[i, pl.ds(ncols, edge)] += shifted(dot_t(g_rows(i, 1, nrows - 1), sw[2]))

    def grad_halo(i):
        gacc[i, pl.ds(0, ncols)] += shifted(dot_t(gp[i, 0], sw[2]))
        gacc[i, pl.ds(edge, ncols)] += shifted(dot_t(gp[i, nrows + 1], sw[0]))

    def grad_full(i):
        wide = dot_t(g_rows(i, 2, nrows), sw[0]) + dot_t(g_rows(i, 1, nrows), sw[1])
        gacc[i] = shifted(wide + dot_t(g_rows(i, 0, nrows), sw[2]))
        grad_done(i)

    def grad_done(i):
        grad = 0.5 * gacc[i]
        gext[i + 1] = grad.astype(BF16)
        gt[:, pl.ds(i * pix, pix)] = grad.T.astype(BF16)

    def outer_sum(i, left, first, count):
        return dot(ft3[:, pl.ds(i * pix + left * ncols, count * ncols)], g_rows(i, first, count))

    def spatial_own(a):
        left, first, count = ((0, 2, nrows - 1), (0, 1, nrows), (1, 1, nrows - 1))[a]
        total = outer_sum(1, left, first, count)
        for i in range(2, npairs - 1):
            total = total + outer_sum(i, left, first, count)
        taps[pl.ds(a * BLOCK, BLOCK)] = total

    def spatial_edge(a):
        left, first = (nrows - 1, nrows + 1) if a == 0 else (0, 0)
        total = taps[pl.ds(a * BLOCK, BLOCK)]
        for i in range(1, npairs - 1):
            total = total + outer_sum(i, left, first, 1)
        taps[pl.ds(a * BLOCK, BLOCK)] = total

    def spatial_rest(a):
        total = taps[pl.ds(a * BLOCK, BLOCK)]
        for i in (0, npairs - 1):
            total = total + outer_sum(i, 0, 2 - a, nrows)
        taps[pl.ds(a * BLOCK, BLOCK)] = total

    def temporal():
        for k in range(3):
            total = dot(gt[:, pl.ds(0, pix)], u[k])
            for i in range(1, npairs):
                total = total + dot(gt[:, pl.ds(i * pix, pix)], u[2 * i + k])
            taps[pl.ds(3 * BLOCK + k * chans, chans)] = total.T

    half = chans // 2
    size = BLOCK // (n * n)
    own_cols = pl.ds(pl.multiple_of(core * half, half), half)
    mate_cols = pl.ds(pl.multiple_of((1 - core) * half, half), half)
    base_z = n * n
    base_g = base_z + nz - 1
    last = base_g + n * n - 1

    def chunk(index):
        return pl.ds(pl.multiple_of(index * size, size), size)

    def link(p, src, dst, slot, device):
        return remote(src, dst, send_sem.at[p], recv_sem.at[p], slot, device)

    def core_copy(p):
        return link(p, sb0.at[p], rb0.at[p], 0, mate)

    def plane_copies(p):
        return [link(p, sb1.at[p, chunk(plane_index(o))], rb1.at[p, o - 1], o, peer_xy(o)) for o in plane]

    def ring_copies(p):
        return [link(p, zb.at[p, z], zb.at[p, z], base_z + o - 1, peer_z(o)) for o in ring]

    def gather_copies(p):
        own = ag.at[p, chunk(chip)]
        return [link(p, own, own, base_g + o - 1, peer_xy(o)) for o in plane]

    def mate_copy(p):
        return link(p, ag.at[p], other.at[p], last, mate)

    def begin(p):
        sb0[p] = taps[pl.ds(p * BLOCK, BLOCK), mate_cols].astype(BF16)
        core_copy(p).start()

    def step_core(p):
        core_copy(p).wait()
        total = taps[pl.ds(p * BLOCK, BLOCK), own_cols] + rb0[p].astype(F32)
        sb1[p] = total.astype(BF16)
        for copy in plane_copies(p):
            copy.start()
        mine = pl.ds(pl.multiple_of(p * BLOCK + chip * size, size), size)
        own1[p] = taps[mine, own_cols] + rb0[p, chunk(chip)].astype(F32)

    def step_plane(p):
        for copy in plane_copies(p):
            copy.wait()
        total = own1[p]
        for o in plane:
            total = total + rb1[p, o - 1].astype(F32)
        zb[p, z] = total.astype(BF16)
        for copy in ring_copies(p):
            copy.start()

    def step_ring(p):
        for copy in ring_copies(p):
            copy.wait()
        total = zb[p, 0].astype(F32)
        for k in range(1, nz):
            total = total + zb[p, k].astype(F32)
        ag[p, chunk(chip)] = total.astype(BF16)
        for copy in gather_copies(p):
            copy.start()

    def finish(p, half_ref, cols):
        value = half_ref[p].astype(F32)
        if p < 3:
            sgrad[pl.ds(p * BLOCK, BLOCK), cols] = value * (0.5 * scale)
        else:
            tgrad[:, cols] = value * scale

    def step_gather(p):
        for copy in gather_copies(p):
            copy.wait()
        mate_copy(p).start()
        finish(p, ag, own_cols)

    def step_mate(p):
        mate_copy(p).wait()
        finish(p, other, mate_cols)

    def put(t, value):
        outs[t] = value.astype(BF16).reshape(nrows, ncols, chans)

    def input_grad(i):
        grad = gext[i + 1]
        base = grad.astype(F32) + dot_t(grad, tw[1])
        first = dot_t(grad, tw[0])
        final = dot_t(grad, tw[2])
        if i == 0:
            part[0] = base + first
        else:
            put(2 * i, base + first + part[2])
            put(2 * i - 1, part[1] + first)
        part[1] = base + final
        part[2] = final

    pass_on(0)
    loads[2].wait()
    loads[3].wait()
    for j in range(1, nframes):
        pair_sum(j)
    hear(0)
    pass_on(1)
    for i in range(1, npairs - 1):
        features(i)
    loads[0].wait()
    loads[1].wait()
    grad_own(0)
    hear(1)
    pass_on(2)
    grad_own(npairs - 1)
    for a in range(3):
        spatial_own(a)
    hear(2)

    rows_down.wait()
    rows_up.wait()

    @pl.when(row == 0)
    def _():
        gp[:, 0] = jnp.zeros((npairs, ncols, chans), BF16)

    @pl.when(row == nrow - 1)
    def _():
        gp[:, nrows + 1] = jnp.zeros((npairs, ncols, chans), BF16)

    for i in (0, npairs - 1):
        grad_halo(i)
        grad_done(i)
    grad_prev = halo(gext.at[1], gext.at[npairs + 1], 4, prv)
    grad_next = halo(gext.at[npairs], gext.at[0], 5, nxt)
    grad_prev.start()
    grad_next.start()
    spatial_edge(0)
    spatial_edge(2)
    x_next.wait()
    x_prev.wait()

    @pl.when(z == 0)
    def _():
        xin[0] = jnp.zeros((nrows, ncols, chans), BF16)

    @pl.when(z == nz - 1)
    def _():
        xin[nframes + 1] = jnp.zeros((nrows, ncols, chans), BF16)

    pair_sum(0)
    pair_sum(nframes)
    features(0)
    features(npairs - 1)
    spatial_rest(0)
    begin(0)
    spatial_rest(1)
    begin(1)
    spatial_rest(2)
    begin(2)
    step_core(0)
    step_core(1)
    step_core(2)
    for i in range(1, npairs - 1):
        grad_full(i)
    temporal()
    begin(3)
    input_grad(0)
    step_core(3)
    step_plane(0)
    input_grad(1)
    step_plane(1)
    input_grad(2)
    step_plane(2)
    input_grad(3)
    step_plane(3)
    step_ring(0)
    step_ring(1)
    step_ring(2)
    step_ring(3)

    grad_prev.wait()
    grad_next.wait()

    @pl.when(z == 0)
    def _():
        gext[0] = jnp.zeros((pix, chans), BF16)

    @pl.when(z == nz - 1)
    def _():
        gext[npairs + 1] = jnp.zeros((pix, chans), BF16)

    put(0, part[0] + dot_t(gext[0], tw[2]))
    put(nframes - 1, part[1] + dot_t(gext[npairs + 1], tw[0]))
    for p in range(PIPES):
        step_gather(p)
        if p:
            step_mate(p - 1)
    step_mate(PIPES - 1)


def write_out(grad, temporal, spatial, grad_hbm, temporal_hbm, spatial_hbm, sems):
    copies = [pltpu.make_async_copy(grad.at[t], grad_hbm.at[t], sems.at[t]) for t in range(grad.shape[0])]
    held, kept = (temporal, spatial), (temporal_hbm, spatial_hbm)
    for part in range(2):
        for k in range(held[part].shape[0]):
            copies.append(pltpu.make_async_copy(held[part].at[k], kept[part].at[k], sems.at[len(copies)]))
    for copy in copies:
        copy.start()
    for copy in copies:
        copy.wait()


def solution(mesh):
    nz = mesh.shape["frame"]
    n = 1
    while 2 * n * n < mesh.shape["row"]:
        n += 1

    def body(inputs, temporal_weight, spatial_weight, pooled_grad):
        nframes, nrows, ncols, chans = inputs.shape
        npairs = nframes // 2
        pix = nrows * ncols
        half = chans // 2
        size = BLOCK // (n * n)
        scale = float(nframes * nz * nrows * mesh.shape["row"] * ncols) ** -0.5
        slots = 2 * n * n + nz - 1
        any_spec = pl.BlockSpec(memory_space=pltpu.HBM)
        vmem_spec = pl.BlockSpec(memory_space=pltpu.VMEM)
        spatial = spatial_weight.reshape(3, 3 * chans, chans)
        input_grad, temporal_grad, spatial_grad = pl.pallas_call(
            functools.partial(kernel, nz, n, scale),
            out_shape=[
                pltpu.VMEM(inputs.shape, BF16),
                pltpu.VMEM((3 * chans, chans), F32),
                pltpu.VMEM((9 * chans, chans), F32),
            ],
            in_specs=[any_spec] * 4,
            out_specs=[vmem_spec] * 3,
            scratch_shapes=[
                pltpu.VMEM((nframes + 2, nrows, ncols, chans), BF16),
                pltpu.VMEM((npairs, nrows + 2, ncols, chans), BF16),
                pltpu.VMEM((3, chans, chans), BF16),
                pltpu.VMEM((3, 3 * chans, chans), BF16),
                pltpu.VMEM((nframes + 1, pix, chans), BF16),
                pltpu.VMEM((npairs, pix, chans), F32),
                pltpu.VMEM((npairs + 2, pix, chans), BF16),
                pltpu.VMEM((3 * chans, npairs * pix), BF16),
                pltpu.VMEM((chans, npairs * pix), BF16),
                pltpu.VMEM((12 * chans, chans), F32),
                pltpu.VMEM((3, pix, chans), F32),
                pltpu.VMEM((PIPES, BLOCK, half), BF16),
                pltpu.VMEM((PIPES, BLOCK, half), BF16),
                pltpu.VMEM((PIPES, BLOCK, half), BF16),
                pltpu.VMEM((PIPES, n * n - 1, size, half), BF16),
                pltpu.VMEM((PIPES, size, half), F32),
                pltpu.VMEM((PIPES, nz, size, half), BF16),
                pltpu.VMEM((PIPES, BLOCK, half), BF16),
                pltpu.VMEM((PIPES, BLOCK, half), BF16),
                pltpu.SemaphoreType.DMA((4,)),
                pltpu.SemaphoreType.DMA((6,)),
                pltpu.SemaphoreType.DMA((6,)),
                pltpu.SemaphoreType.DMA((PIPES, slots)),
                pltpu.SemaphoreType.DMA((PIPES, slots)),
                pltpu.SemaphoreType.REGULAR((3,)),
            ],
            compiler_params=pltpu.CompilerParams(
                collective_id=0, has_side_effects=True, vmem_limit_bytes=58 * 1024 * 1024),
            cost_estimate=pl.CostEstimate(
                flops=28 * 2 * npairs * pix * chans * chans, bytes_accessed=10 * 2**20, transcendentals=0),
            name="block",
        )(inputs, temporal_weight, spatial, pooled_grad)
        input_grad, temporal_grad, spatial_grad = pl.pallas_call(
            write_out,
            out_shape=[
                jax.ShapeDtypeStruct(inputs.shape, BF16),
                jax.ShapeDtypeStruct((3, chans, chans), F32),
                jax.ShapeDtypeStruct((9, chans, chans), F32),
            ],
            in_specs=[pl.BlockSpec(memory_space=pl.ANY)] * 3,
            out_specs=[any_spec] * 3,
            scratch_shapes=[pltpu.SemaphoreType.DMA((nframes + 12,))],
            compiler_params=pltpu.CompilerParams(vmem_limit_bytes=2**20),
            name="write_out",
        )(input_grad, temporal_grad.reshape(3, chans, chans), spatial_grad.reshape(9, chans, chans))
        return input_grad, temporal_grad, spatial_grad.reshape(3, 3, chans, chans)

    in_specs = (P("frame", "row", None, None), P(), P(), P("frame", "row", None, None))
    out_specs = (P("frame", "row", None, None), P(), P())
    return jax.shard_map(body, mesh=mesh, in_specs=in_specs, out_specs=out_specs, check_vma=False)
```

```python
import functools

import jax
import jax.numpy as jnp
from jax import lax
from jax.experimental import pallas as pl
from jax.experimental.pallas import tpu as pltpu
from jax.sharding import PartitionSpec as P

MESH = pl.DeviceIdType.MESH
F32 = jnp.float32
BF16 = jnp.bfloat16
PIPES = 4
BLOCK = 768


def dot(left, right):
    return jnp.dot(left, right, preferred_element_type=F32)


def dot_t(left, right):
    return lax.dot_general(left, right, (((1,), (1,)), ((), ())), preferred_element_type=F32)


def kernel(nz, n, scale, x_hbm, tw_hbm, sw_hbm, g_hbm, outs, tgrad, sgrad,
           xin, gp, tw, sw, u, gacc, gext, ft3, gt, taps, part,
           sb0, rb0, sb1, rb1, own1, zb, ag, other,
           local_sem, halo_send, halo_recv, send_sem, recv_sem, relay):
    nframes, nrows, ncols, chans = x_hbm.shape
    npairs = nframes // 2
    pix = nrows * ncols
    z = lax.axis_index("frame")
    row = lax.axis_index("row")
    nrow = 2 * n * n
    core = row % 2
    y = (row // 2) % n
    x = row // (2 * n)
    chip = row // 2
    mate = (z, row + 1 - 2 * core)

    def plane_index(o):
        return (x + o // n) % n * n + (y + o % n) % n

    def peer_xy(o):
        return (z, 2 * plane_index(o) + core)

    def peer_z(o):
        return ((z + o) % nz, row)

    plane = sorted(range(1, n * n), key=lambda o: -min(o // n, n - o // n) - min(o % n, n - o % n))
    ring = sorted(range(1, nz), key=lambda o: -min(o, nz - o))
    down, up = (z, (row + 1) % nrow), (z, (row + nrow - 1) % nrow)
    nxt, prv = peer_z(1), peer_z(nz - 1)

    loads = [
        pltpu.make_async_copy(g_hbm, gp.at[:, pl.ds(1, nrows)], local_sem.at[0]),
        pltpu.make_async_copy(sw_hbm, sw, local_sem.at[1]),
        pltpu.make_async_copy(tw_hbm, tw, local_sem.at[2]),
        pltpu.make_async_copy(x_hbm, xin.at[pl.ds(1, nframes)], local_sem.at[3]),
    ]
    barrier = pltpu.get_barrier_semaphore()
    outer = (z, (row + nrow + 2 * core - 1) % nrow)
    around = [peer_xy(1), peer_xy(n - 1), peer_xy(n), peer_xy(n * (n - 1)), nxt, prv]
    for device in [mate, outer] + around:
        pl.semaphore_signal(barrier, inc=1, device_id=device, device_id_type=MESH)
    for k in (3, 2, 0, 1):
        loads[k].start()
    pl.semaphore_wait(barrier, 2 + len(around))

    def pass_on(k):
        for device in around:
            pl.semaphore_signal(relay.at[k], inc=1, device_id=device, device_id_type=MESH)

    def hear(k):
        pl.semaphore_wait(relay.at[k], len(around))

    def remote(src, dst, sends, recvs, slot, device):
        return pltpu.make_async_remote_copy(
            src_ref=src, dst_ref=dst, send_sem=sends.at[slot], recv_sem=recvs.at[slot],
            device_id=device, device_id_type=MESH)

    def halo(src, dst, slot, device):
        return remote(src, dst, halo_send, halo_recv, slot, device)

    x_next = halo(x_hbm.at[nframes - 1], xin.at[0], 2, nxt)
    x_prev = halo(x_hbm.at[0], xin.at[nframes + 1], 3, prv)
    rows_down = halo(g_hbm.at[:, nrows - 1], gp.at[:, 0], 0, down)
    rows_up = halo(g_hbm.at[:, 0], gp.at[:, nrows + 1], 1, up)
    for copy in (x_next, x_prev, rows_down, rows_up):
        copy.start()

    def frame(i):
        return xin[i].reshape(pix, chans)

    lane = lax.broadcasted_iota(jnp.int32, (chans, pix), 1) % ncols

    def pair_sum(j):
        u[j] = (frame(j).astype(F32) + frame(j + 1).astype(F32)).astype(BF16)

    def features(i):
        total = dot(u[2 * i], tw[0]) + dot(u[2 * i + 1], tw[1]) + dot(u[2 * i + 2], tw[2])
        total = total + (frame(2 * i + 1).astype(F32) + frame(2 * i + 2).astype(F32))
        flip = total.T
        at = pl.ds(i * pix, pix)
        ft3[pl.ds(chans, chans), at] = flip.astype(BF16)
        right = jnp.where(lane == 0, 0.0, pltpu.roll(flip, 1, 1))
        ft3[pl.ds(0, chans), at] = right.astype(BF16)
        left = jnp.where(lane == ncols - 1, 0.0, pltpu.roll(flip, pix - 1, 1))
        ft3[pl.ds(2 * chans, chans), at] = left.astype(BF16)

    def g_rows(i, first, count):
        return gp[i, pl.ds(first, count)].reshape(count * ncols, chans)

    def shifted(wide):
        column = lax.broadcasted_iota(jnp.int32, (wide.shape[0], chans), 0) % ncols
        low, mid, high = (wide[:, b * chans:(b + 1) * chans] for b in range(3))
        low = jnp.where(column == ncols - 1, 0.0, pltpu.roll(low, wide.shape[0] - 1, 0))
        high = jnp.where(column == 0, 0.0, pltpu.roll(high, 1, 0))
        return low + mid + high

    edge = pix - ncols

    def grad_own(i):
        gacc[i] = shifted(dot_t(g_rows(i, 1, nrows), sw[1]))
        gacc[i, pl.ds(0, edge)] += shifted(dot_t(g_rows(i, 2, nrows - 1), sw[0]))
        gacc[i, pl.ds(ncols, edge)] += shifted(dot_t(g_rows(i, 1, nrows - 1), sw[2]))

    def grad_halo():
        first = shifted(dot_t(gp[:, 0].reshape(npairs * ncols, chans), sw[2]))
        final = shifted(dot_t(gp[:, nrows + 1].reshape(npairs * ncols, chans), sw[0]))
        for i in range(npairs):
            gacc[i, pl.ds(0, ncols)] += first[i * ncols:(i + 1) * ncols]
            gacc[i, pl.ds(edge, ncols)] += final[i * ncols:(i + 1) * ncols]

    def grad_done(i):
        grad = 0.5 * gacc[i]
        gext[i + 1] = grad.astype(BF16)
        gt[:, pl.ds(i * pix, pix)] = grad.T.astype(BF16)

    def outer_sum(i, left, first, count):
        return dot(ft3[:, pl.ds(i * pix + left * ncols, count * ncols)], g_rows(i, first, count))

    def spatial_own(a):
        left, first, count = ((0, 2, nrows - 1), (0, 1, nrows), (1, 1, nrows - 1))[a]
        total = outer_sum(1, left, first, count)
        for i in range(2, npairs - 1):
            total = total + outer_sum(i, left, first, count)
        taps[pl.ds(a * BLOCK, BLOCK)] = total

    def spatial_rest(a):
        total = taps[pl.ds(a * BLOCK, BLOCK)]
        for i in range(1, npairs - 1):
            if a == 0:
                total = total + outer_sum(i, nrows - 1, nrows + 1, 1)
            if a == 2:
                total = total + outer_sum(i, 0, 0, 1)
        for i in (0, npairs - 1):
            total = total + outer_sum(i, 0, 2 - a, nrows)
        taps[pl.ds(a * BLOCK, BLOCK)] = total

    def temporal():
        for k in range(3):
            total = dot(gt[:, pl.ds(0, pix)], u[k])
            for i in range(1, npairs):
                total = total + dot(gt[:, pl.ds(i * pix, pix)], u[2 * i + k])
            taps[pl.ds(3 * BLOCK + k * chans, chans)] = total.T

    half = chans // 2
    size = BLOCK // (n * n)
    own_cols = pl.ds(pl.multiple_of(core * half, half), half)
    mate_cols = pl.ds(pl.multiple_of((1 - core) * half, half), half)
    base_z = n * n
    base_g = base_z + nz - 1
    last = base_g + n * n - 1

    def chunk(index):
        return pl.ds(pl.multiple_of(index * size, size), size)

    def link(p, src, dst, slot, device):
        return remote(src, dst, send_sem.at[p], recv_sem.at[p], slot, device)

    def core_copy(p):
        return link(p, sb0.at[p], rb0.at[p], 0, mate)

    def plane_copies(p):
        return [link(p, sb1.at[p, chunk(plane_index(o))], rb1.at[p, o - 1], o, peer_xy(o)) for o in plane]

    def ring_copies(p):
        return [link(p, zb.at[p, z], zb.at[p, z], base_z + o - 1, peer_z(o)) for o in ring]

    def gather_copies(p):
        own = ag.at[p, chunk(chip)]
        return [link(p, own, own, base_g + o - 1, peer_xy(o)) for o in plane]

    def mate_copy(p):
        return link(p, ag.at[p], other.at[p], last, mate)

    def begin(p):
        sb0[p] = taps[pl.ds(p * BLOCK, BLOCK), mate_cols].astype(BF16)
        core_copy(p).start()

    def step_core(p):
        core_copy(p).wait()
        total = taps[pl.ds(p * BLOCK, BLOCK), own_cols] + rb0[p].astype(F32)
        sb1[p] = total.astype(BF16)
        for copy in plane_copies(p):
            copy.start()
        mine = pl.ds(pl.multiple_of(p * BLOCK + chip * size, size), size)
        own1[p] = taps[mine, own_cols] + rb0[p, chunk(chip)].astype(F32)

    def step_plane(p):
        for copy in plane_copies(p):
            copy.wait()
        total = own1[p]
        for o in plane:
            total = total + rb1[p, o - 1].astype(F32)
        zb[p, z] = total.astype(BF16)
        for copy in ring_copies(p):
            copy.start()

    def step_ring(p):
        for copy in ring_copies(p):
            copy.wait()
        total = zb[p, 0].astype(F32)
        for k in range(1, nz):
            total = total + zb[p, k].astype(F32)
        ag[p, chunk(chip)] = total.astype(BF16)
        for copy in gather_copies(p):
            copy.start()

    def finish(p, half_ref, cols):
        value = half_ref[p].astype(F32)
        if p < 3:
            sgrad[pl.ds(p * BLOCK, BLOCK), cols] = value * (0.5 * scale)
        else:
            tgrad[:, cols] = value * scale

    def step_gather(p):
        for copy in gather_copies(p):
            copy.wait()
        mate_copy(p).start()
        finish(p, ag, own_cols)

    def step_mate(p):
        mate_copy(p).wait()
        finish(p, other, mate_cols)

    def put(t, value):
        outs[t] = value.astype(BF16).reshape(nrows, ncols, chans)

    def input_grad(i):
        grad = gext[i + 1]
        base = grad.astype(F32) + dot_t(grad, tw[1])
        first = dot_t(grad, tw[0])
        final = dot_t(grad, tw[2])
        if i == 0:
            part[0] = base + first
        else:
            put(2 * i, base + first + part[2])
            put(2 * i - 1, part[1] + first)
        part[1] = base + final
        part[2] = final

    pass_on(0)
    loads[2].wait()
    loads[3].wait()
    for j in range(1, nframes):
        pair_sum(j)
    hear(0)
    pass_on(1)
    for i in range(1, npairs - 1):
        features(i)
    loads[0].wait()
    loads[1].wait()
    grad_own(0)
    hear(1)
    pass_on(2)
    for i in range(1, npairs):
        grad_own(i)
    for a in range(3):
        spatial_own(a)
    hear(2)

    rows_down.wait()
    rows_up.wait()

    @pl.when(row == 0)
    def _():
        gp[:, 0] = jnp.zeros((npairs, ncols, chans), BF16)

    @pl.when(row == nrow - 1)
    def _():
        gp[:, nrows + 1] = jnp.zeros((npairs, ncols, chans), BF16)

    grad_halo()
    grad_done(0)
    grad_done(npairs - 1)
    grad_prev = halo(gext.at[1], gext.at[npairs + 1], 4, prv)
    grad_next = halo(gext.at[npairs], gext.at[0], 5, nxt)
    grad_prev.start()
    grad_next.start()
    x_next.wait()
    x_prev.wait()

    @pl.when(z == 0)
    def _():
        xin[0] = jnp.zeros((nrows, ncols, chans), BF16)

    @pl.when(z == nz - 1)
    def _():
        xin[nframes + 1] = jnp.zeros((nrows, ncols, chans), BF16)

    pair_sum(0)
    pair_sum(nframes)
    features(0)
    features(npairs - 1)
    spatial_rest(0)
    begin(0)
    spatial_rest(1)
    begin(1)
    step_core(0)
    spatial_rest(2)
    begin(2)
    step_core(1)
    for i in range(1, npairs - 1):
        grad_done(i)
    step_core(2)
    temporal()
    begin(3)
    input_grad(0)
    step_core(3)
    step_plane(0)
    input_grad(1)
    step_plane(1)
    input_grad(2)
    step_plane(2)
    input_grad(3)
    step_plane(3)
    step_ring(0)
    step_ring(1)
    step_ring(2)
    step_ring(3)

    grad_prev.wait()
    grad_next.wait()

    @pl.when(z == 0)
    def _():
        gext[0] = jnp.zeros((pix, chans), BF16)

    @pl.when(z == nz - 1)
    def _():
        gext[npairs + 1] = jnp.zeros((pix, chans), BF16)

    put(0, part[0] + dot_t(gext[0], tw[2]))
    put(nframes - 1, part[1] + dot_t(gext[npairs + 1], tw[0]))
    for p in range(PIPES):
        step_gather(p)
        if p:
            step_mate(p - 1)
    step_mate(PIPES - 1)


def write_out(grad, temporal, spatial, grad_hbm, temporal_hbm, spatial_hbm, sems):
    copies = [pltpu.make_async_copy(grad.at[t], grad_hbm.at[t], sems.at[t]) for t in range(grad.shape[0])]
    held, kept = (temporal, spatial), (temporal_hbm, spatial_hbm)
    for part in range(2):
        for k in range(held[part].shape[0]):
            copies.append(pltpu.make_async_copy(held[part].at[k], kept[part].at[k], sems.at[len(copies)]))
    for copy in copies:
        copy.start()
    for copy in copies:
        copy.wait()


def solution(mesh):
    nz = mesh.shape["frame"]
    n = 1
    while 2 * n * n < mesh.shape["row"]:
        n += 1

    def body(inputs, temporal_weight, spatial_weight, pooled_grad):
        nframes, nrows, ncols, chans = inputs.shape
        npairs = nframes // 2
        pix = nrows * ncols
        half = chans // 2
        size = BLOCK // (n * n)
        scale = float(nframes * nz * nrows * mesh.shape["row"] * ncols) ** -0.5
        slots = 2 * n * n + nz - 1
        any_spec = pl.BlockSpec(memory_space=pltpu.HBM)
        vmem_spec = pl.BlockSpec(memory_space=pltpu.VMEM)
        spatial = spatial_weight.reshape(3, 3 * chans, chans)
        input_grad, temporal_grad, spatial_grad = pl.pallas_call(
            functools.partial(kernel, nz, n, scale),
            out_shape=[
                pltpu.VMEM(inputs.shape, BF16),
                pltpu.VMEM((3 * chans, chans), F32),
                pltpu.VMEM((9 * chans, chans), F32),
            ],
            in_specs=[any_spec] * 4,
            out_specs=[vmem_spec] * 3,
            scratch_shapes=[
                pltpu.VMEM((nframes + 2, nrows, ncols, chans), BF16),
                pltpu.VMEM((npairs, nrows + 2, ncols, chans), BF16),
                pltpu.VMEM((3, chans, chans), BF16),
                pltpu.VMEM((3, 3 * chans, chans), BF16),
                pltpu.VMEM((nframes + 1, pix, chans), BF16),
                pltpu.VMEM((npairs, pix, chans), F32),
                pltpu.VMEM((npairs + 2, pix, chans), BF16),
                pltpu.VMEM((3 * chans, npairs * pix), BF16),
                pltpu.VMEM((chans, npairs * pix), BF16),
                pltpu.VMEM((12 * chans, chans), F32),
                pltpu.VMEM((3, pix, chans), F32),
                pltpu.VMEM((PIPES, BLOCK, half), BF16),
                pltpu.VMEM((PIPES, BLOCK, half), BF16),
                pltpu.VMEM((PIPES, BLOCK, half), BF16),
                pltpu.VMEM((PIPES, n * n - 1, size, half), BF16),
                pltpu.VMEM((PIPES, size, half), F32),
                pltpu.VMEM((PIPES, nz, size, half), BF16),
                pltpu.VMEM((PIPES, BLOCK, half), BF16),
                pltpu.VMEM((PIPES, BLOCK, half), BF16),
                pltpu.SemaphoreType.DMA((4,)),
                pltpu.SemaphoreType.DMA((6,)),
                pltpu.SemaphoreType.DMA((6,)),
                pltpu.SemaphoreType.DMA((PIPES, slots)),
                pltpu.SemaphoreType.DMA((PIPES, slots)),
                pltpu.SemaphoreType.REGULAR((3,)),
            ],
            compiler_params=pltpu.CompilerParams(
                collective_id=0, has_side_effects=True, vmem_limit_bytes=58 * 1024 * 1024),
            cost_estimate=pl.CostEstimate(
                flops=28 * 2 * npairs * pix * chans * chans, bytes_accessed=10 * 2**20, transcendentals=0),
            name="block",
        )(inputs, temporal_weight, spatial, pooled_grad)
        input_grad, temporal_grad, spatial_grad = pl.pallas_call(
            write_out,
            out_shape=[
                jax.ShapeDtypeStruct(inputs.shape, BF16),
                jax.ShapeDtypeStruct((3, chans, chans), F32),
                jax.ShapeDtypeStruct((9, chans, chans), F32),
            ],
            in_specs=[pl.BlockSpec(memory_space=pl.ANY)] * 3,
            out_specs=[any_spec] * 3,
            scratch_shapes=[pltpu.SemaphoreType.DMA((nframes + 12,))],
            compiler_params=pltpu.CompilerParams(vmem_limit_bytes=2**20),
            name="write_out",
        )(input_grad, temporal_grad.reshape(3, chans, chans), spatial_grad.reshape(9, chans, chans))
        return input_grad, temporal_grad, spatial_grad.reshape(3, 3, chans, chans)

    in_specs = (P("frame", "row", None, None), P(), P(), P("frame", "row", None, None))
    out_specs = (P("frame", "row", None, None), P(), P())
    return jax.shard_map(body, mesh=mesh, in_specs=in_specs, out_specs=out_specs, check_vma=False)
```

```python
import functools

import jax
import jax.numpy as jnp
from jax import lax
from jax.experimental import pallas as pl
from jax.experimental.pallas import tpu as pltpu
from jax.sharding import PartitionSpec as P

MESH = pl.DeviceIdType.MESH
F32 = jnp.float32
BF16 = jnp.bfloat16
PIPES = 4
BLOCK = 768


def dot(left, right):
    return jnp.dot(left, right, preferred_element_type=F32)


def dot_t(left, right):
    return lax.dot_general(left, right, (((1,), (1,)), ((), ())), preferred_element_type=F32)


def kernel(nz, n, scale, x_hbm, tw_hbm, sw_hbm, g_hbm, outs, tgrad, sgrad,
           xin, gp, tw, sw, u, gacc, gext, ft3, gt, taps, part,
           sb0, rb0, sb1, rb1, own1, zb, ag, other,
           local_sem, halo_send, halo_recv, send_sem, recv_sem, relay):
    nframes, nrows, ncols, chans = x_hbm.shape
    npairs = nframes // 2
    pix = nrows * ncols
    z = lax.axis_index("frame")
    row = lax.axis_index("row")
    nrow = 2 * n * n
    core = row % 2
    y = (row // 2) % n
    x = row // (2 * n)
    chip = row // 2
    mate = (z, row + 1 - 2 * core)

    def plane_index(o):
        return (x + o // n) % n * n + (y + o % n) % n

    def peer_xy(o):
        return (z, 2 * plane_index(o) + core)

    def peer_z(o):
        return ((z + o) % nz, row)

    plane = sorted(range(1, n * n), key=lambda o: -min(o // n, n - o // n) - min(o % n, n - o % n))
    ring = sorted(range(1, nz), key=lambda o: -min(o, nz - o))
    down, up = (z, (row + 1) % nrow), (z, (row + nrow - 1) % nrow)
    nxt, prv = peer_z(1), peer_z(nz - 1)

    loads = [
        pltpu.make_async_copy(g_hbm, gp.at[:, pl.ds(1, nrows)], local_sem.at[0]),
        pltpu.make_async_copy(sw_hbm, sw, local_sem.at[1]),
        pltpu.make_async_copy(tw_hbm, tw, local_sem.at[2]),
        pltpu.make_async_copy(x_hbm, xin.at[pl.ds(1, nframes)], local_sem.at[3]),
    ]
    barrier = pltpu.get_barrier_semaphore()
    outer = (z, (row + nrow + 2 * core - 1) % nrow)
    around = [peer_xy(1), peer_xy(n - 1), peer_xy(n), peer_xy(n * (n - 1)), nxt, prv]
    for device in [mate, outer] + around:
        pl.semaphore_signal(barrier, inc=1, device_id=device, device_id_type=MESH)
    for k in (3, 2, 0, 1):
        loads[k].start()
    pl.semaphore_wait(barrier, 2 + len(around))

    def pass_on(k):
        for device in around:
            pl.semaphore_signal(relay.at[k], inc=1, device_id=device, device_id_type=MESH)

    def hear(k):
        pl.semaphore_wait(relay.at[k], len(around))

    def remote(src, dst, sends, recvs, slot, device):
        return pltpu.make_async_remote_copy(
            src_ref=src, dst_ref=dst, send_sem=sends.at[slot], recv_sem=recvs.at[slot],
            device_id=device, device_id_type=MESH)

    def halo(src, dst, slot, device):
        return remote(src, dst, halo_send, halo_recv, slot, device)

    x_next = halo(x_hbm.at[nframes - 1], xin.at[0], 2, nxt)
    x_prev = halo(x_hbm.at[0], xin.at[nframes + 1], 3, prv)
    rows_down = halo(g_hbm.at[:, nrows - 1], gp.at[:, 0], 0, down)
    rows_up = halo(g_hbm.at[:, 0], gp.at[:, nrows + 1], 1, up)
    for copy in (x_next, x_prev, rows_down, rows_up):
        copy.start()

    def frame(i):
        return xin[i].reshape(pix, chans)

    lane = lax.broadcasted_iota(jnp.int32, (chans, pix), 1) % ncols

    def pair_sum(j):
        u[j] = (frame(j).astype(F32) + frame(j + 1).astype(F32)).astype(BF16)

    def features(i):
        total = dot(u[2 * i], tw[0]) + dot(u[2 * i + 1], tw[1]) + dot(u[2 * i + 2], tw[2])
        total = total + (frame(2 * i + 1).astype(F32) + frame(2 * i + 2).astype(F32))
        flip = total.T
        at = pl.ds(i * pix, pix)
        ft3[pl.ds(chans, chans), at] = flip.astype(BF16)
        right = jnp.where(lane == 0, 0.0, pltpu.roll(flip, 1, 1))
        ft3[pl.ds(0, chans), at] = right.astype(BF16)
        left = jnp.where(lane == ncols - 1, 0.0, pltpu.roll(flip, pix - 1, 1))
        ft3[pl.ds(2 * chans, chans), at] = left.astype(BF16)

    def g_rows(i, first, count):
        return gp[i, pl.ds(first, count)].reshape(count * ncols, chans)

    def shifted(wide):
        column = lax.broadcasted_iota(jnp.int32, (wide.shape[0], chans), 0) % ncols
        low, mid, high = (wide[:, b * chans:(b + 1) * chans] for b in range(3))
        low = jnp.where(column == ncols - 1, 0.0, pltpu.roll(low, wide.shape[0] - 1, 0))
        high = jnp.where(column == 0, 0.0, pltpu.roll(high, 1, 0))
        return low + mid + high

    edge = pix - ncols

    def grad_own(i):
        gacc[i] = shifted(dot_t(g_rows(i, 1, nrows), sw[1]))
        gacc[i, pl.ds(0, edge)] += shifted(dot_t(g_rows(i, 2, nrows - 1), sw[0]))
        gacc[i, pl.ds(ncols, edge)] += shifted(dot_t(g_rows(i, 1, nrows - 1), sw[2]))

    def grad_halo(i):
        gacc[i, pl.ds(0, ncols)] += shifted(dot_t(gp[i, 0], sw[2]))
        gacc[i, pl.ds(edge, ncols)] += shifted(dot_t(gp[i, nrows + 1], sw[0]))

    def grad_full(i):
        wide = dot_t(g_rows(i, 2, nrows), sw[0]) + dot_t(g_rows(i, 1, nrows), sw[1])
        gacc[i] = shifted(wide + dot_t(g_rows(i, 0, nrows), sw[2]))
        grad_done(i)

    def grad_done(i):
        grad = 0.5 * gacc[i]
        gext[i + 1] = grad.astype(BF16)
        gt[:, pl.ds(i * pix, pix)] = grad.T.astype(BF16)

    def outer_sum(i, left, first, count):
        return dot(ft3[:, pl.ds(i * pix + left * ncols, count * ncols)], g_rows(i, first, count))

    def spatial_own(a):
        left, first, count = ((0, 2, nrows - 1), (0, 1, nrows), (1, 1, nrows - 1))[a]
        total = outer_sum(1, left, first, count)
        for i in range(2, npairs - 1):
            total = total + outer_sum(i, left, first, count)
        taps[pl.ds(a * BLOCK, BLOCK)] = total

    def spatial_edge(a):
        left, first = (nrows - 1, nrows + 1) if a == 0 else (0, 0)
        total = taps[pl.ds(a * BLOCK, BLOCK)]
        for i in range(1, npairs - 1):
            total = total + outer_sum(i, left, first, 1)
        taps[pl.ds(a * BLOCK, BLOCK)] = total

    def spatial_rest(a):
        total = taps[pl.ds(a * BLOCK, BLOCK)]
        for i in (0, npairs - 1):
            total = total + outer_sum(i, 0, 2 - a, nrows)
        taps[pl.ds(a * BLOCK, BLOCK)] = total

    def temporal():
        for k in range(3):
            total = dot(gt[:, pl.ds(0, pix)], u[k])
            for i in range(1, npairs):
                total = total + dot(gt[:, pl.ds(i * pix, pix)], u[2 * i + k])
            taps[pl.ds(3 * BLOCK + k * chans, chans)] = total.T

    half = chans // 2
    size = BLOCK // (n * n)
    own_cols = pl.ds(pl.multiple_of(core * half, half), half)
    mate_cols = pl.ds(pl.multiple_of((1 - core) * half, half), half)
    base_z = n * n
    base_g = base_z + nz - 1
    last = base_g + n * n - 1

    def chunk(index):
        return pl.ds(pl.multiple_of(index * size, size), size)

    def link(p, src, dst, slot, device):
        return remote(src, dst, send_sem.at[p], recv_sem.at[p], slot, device)

    def core_copy(p):
        return link(p, sb0.at[p], rb0.at[p], 0, mate)

    def plane_copies(p):
        return [link(p, sb1.at[p, chunk(plane_index(o))], rb1.at[p, o - 1], o, peer_xy(o)) for o in plane]

    def ring_copies(p):
        return [link(p, zb.at[p, z], zb.at[p, z], base_z + o - 1, peer_z(o)) for o in ring]

    def gather_copies(p):
        own = ag.at[p, chunk(chip)]
        return [link(p, own, own, base_g + o - 1, peer_xy(o)) for o in plane]

    def mate_copy(p):
        return link(p, ag.at[p], other.at[p], last, mate)

    def begin(p):
        sb0[p] = taps[pl.ds(p * BLOCK, BLOCK), mate_cols].astype(BF16)
        core_copy(p).start()

    def step_core(p):
        core_copy(p).wait()
        total = taps[pl.ds(p * BLOCK, BLOCK), own_cols] + rb0[p].astype(F32)
        sb1[p] = total.astype(BF16)
        for copy in plane_copies(p):
            copy.start()
        mine = pl.ds(pl.multiple_of(p * BLOCK + chip * size, size), size)
        own1[p] = taps[mine, own_cols] + rb0[p, chunk(chip)].astype(F32)

    def step_plane(p):
        for copy in plane_copies(p):
            copy.wait()
        total = own1[p]
        for o in plane:
            total = total + rb1[p, o - 1].astype(F32)
        zb[p, z] = total.astype(BF16)
        for copy in ring_copies(p):
            copy.start()

    def step_ring(p):
        for copy in ring_copies(p):
            copy.wait()
        total = zb[p, 0].astype(F32)
        for k in range(1, nz):
            total = total + zb[p, k].astype(F32)
        ag[p, chunk(chip)] = total.astype(BF16)
        for copy in gather_copies(p):
            copy.start()

    def finish(p, half_ref, cols):
        value = half_ref[p].astype(F32)
        if p < 3:
            sgrad[pl.ds(p * BLOCK, BLOCK), cols] = value * (0.5 * scale)
        else:
            tgrad[:, cols] = value * scale

    def step_gather(p):
        for copy in gather_copies(p):
            copy.wait()
        mate_copy(p).start()
        finish(p, ag, own_cols)

    def step_mate(p):
        mate_copy(p).wait()
        finish(p, other, mate_cols)

    def put(t, value):
        outs[t] = value.astype(BF16).reshape(nrows, ncols, chans)

    def input_grad(i):
        grad = gext[i + 1]
        base = grad.astype(F32) + dot_t(grad, tw[1])
        first = dot_t(grad, tw[0])
        final = dot_t(grad, tw[2])
        if i == 0:
            part[0] = base + first
        else:
            put(2 * i, base + first + part[2])
            put(2 * i - 1, part[1] + first)
        part[1] = base + final
        part[2] = final

    pass_on(0)
    loads[2].wait()
    loads[3].wait()
    for j in range(1, nframes):
        pair_sum(j)
    hear(0)
    pass_on(1)
    for i in range(1, npairs - 1):
        features(i)
    loads[0].wait()
    loads[1].wait()
    grad_own(0)
    hear(1)
    pass_on(2)
    grad_own(npairs - 1)
    for a in range(3):
        spatial_own(a)
    hear(2)

    rows_down.wait()
    rows_up.wait()

    @pl.when(row == 0)
    def _():
        gp[:, 0] = jnp.zeros((npairs, ncols, chans), BF16)

    @pl.when(row == nrow - 1)
    def _():
        gp[:, nrows + 1] = jnp.zeros((npairs, ncols, chans), BF16)

    for i in (0, npairs - 1):
        grad_halo(i)
        grad_done(i)
    grad_prev = halo(gext.at[1], gext.at[npairs + 1], 4, prv)
    grad_next = halo(gext.at[npairs], gext.at[0], 5, nxt)
    grad_prev.start()
    grad_next.start()
    spatial_edge(0)
    spatial_edge(2)
    x_next.wait()
    x_prev.wait()

    @pl.when(z == 0)
    def _():
        xin[0] = jnp.zeros((nrows, ncols, chans), BF16)

    @pl.when(z == nz - 1)
    def _():
        xin[nframes + 1] = jnp.zeros((nrows, ncols, chans), BF16)

    pair_sum(0)
    pair_sum(nframes)
    features(0)
    features(npairs - 1)
    spatial_rest(0)
    begin(0)
    spatial_rest(1)
    begin(1)
    step_core(0)
    spatial_rest(2)
    begin(2)
    step_core(1)
    for i in range(1, npairs - 1):
        grad_full(i)
    step_core(2)
    temporal()
    begin(3)
    input_grad(0)
    step_core(3)
    step_plane(0)
    input_grad(1)
    step_plane(1)
    input_grad(2)
    step_plane(2)
    input_grad(3)
    step_plane(3)
    step_ring(0)
    step_ring(1)
    step_ring(2)
    step_ring(3)

    grad_prev.wait()
    grad_next.wait()

    @pl.when(z == 0)
    def _():
        gext[0] = jnp.zeros((pix, chans), BF16)

    @pl.when(z == nz - 1)
    def _():
        gext[npairs + 1] = jnp.zeros((pix, chans), BF16)

    put(0, part[0] + dot_t(gext[0], tw[2]))
    put(nframes - 1, part[1] + dot_t(gext[npairs + 1], tw[0]))
    for p in range(PIPES):
        step_gather(p)
        if p:
            step_mate(p - 1)
    step_mate(PIPES - 1)


def write_out(grad, temporal, spatial, grad_hbm, temporal_hbm, spatial_hbm, sems):
    copies = [pltpu.make_async_copy(grad.at[t], grad_hbm.at[t], sems.at[t]) for t in range(grad.shape[0])]
    held, kept = (temporal, spatial), (temporal_hbm, spatial_hbm)
    for part in range(2):
        for k in range(held[part].shape[0]):
            copies.append(pltpu.make_async_copy(held[part].at[k], kept[part].at[k], sems.at[len(copies)]))
    for copy in copies:
        copy.start()
    for copy in copies:
        copy.wait()


def solution(mesh):
    nz = mesh.shape["frame"]
    n = 1
    while 2 * n * n < mesh.shape["row"]:
        n += 1

    def body(inputs, temporal_weight, spatial_weight, pooled_grad):
        nframes, nrows, ncols, chans = inputs.shape
        npairs = nframes // 2
        pix = nrows * ncols
        half = chans // 2
        size = BLOCK // (n * n)
        scale = float(nframes * nz * nrows * mesh.shape["row"] * ncols) ** -0.5
        slots = 2 * n * n + nz - 1
        any_spec = pl.BlockSpec(memory_space=pltpu.HBM)
        vmem_spec = pl.BlockSpec(memory_space=pltpu.VMEM)
        spatial = spatial_weight.reshape(3, 3 * chans, chans)
        input_grad, temporal_grad, spatial_grad = pl.pallas_call(
            functools.partial(kernel, nz, n, scale),
            out_shape=[
                pltpu.VMEM(inputs.shape, BF16),
                pltpu.VMEM((3 * chans, chans), F32),
                pltpu.VMEM((9 * chans, chans), F32),
            ],
            in_specs=[any_spec] * 4,
            out_specs=[vmem_spec] * 3,
            scratch_shapes=[
                pltpu.VMEM((nframes + 2, nrows, ncols, chans), BF16),
                pltpu.VMEM((npairs, nrows + 2, ncols, chans), BF16),
                pltpu.VMEM((3, chans, chans), BF16),
                pltpu.VMEM((3, 3 * chans, chans), BF16),
                pltpu.VMEM((nframes + 1, pix, chans), BF16),
                pltpu.VMEM((npairs, pix, chans), F32),
                pltpu.VMEM((npairs + 2, pix, chans), BF16),
                pltpu.VMEM((3 * chans, npairs * pix), BF16),
                pltpu.VMEM((chans, npairs * pix), BF16),
                pltpu.VMEM((12 * chans, chans), F32),
                pltpu.VMEM((3, pix, chans), F32),
                pltpu.VMEM((PIPES, BLOCK, half), BF16),
                pltpu.VMEM((PIPES, BLOCK, half), BF16),
                pltpu.VMEM((PIPES, BLOCK, half), BF16),
                pltpu.VMEM((PIPES, n * n - 1, size, half), BF16),
                pltpu.VMEM((PIPES, size, half), F32),
                pltpu.VMEM((PIPES, nz, size, half), BF16),
                pltpu.VMEM((PIPES, BLOCK, half), BF16),
                pltpu.VMEM((PIPES, BLOCK, half), BF16),
                pltpu.SemaphoreType.DMA((4,)),
                pltpu.SemaphoreType.DMA((6,)),
                pltpu.SemaphoreType.DMA((6,)),
                pltpu.SemaphoreType.DMA((PIPES, slots)),
                pltpu.SemaphoreType.DMA((PIPES, slots)),
                pltpu.SemaphoreType.REGULAR((3,)),
            ],
            compiler_params=pltpu.CompilerParams(
                collective_id=0, has_side_effects=True, vmem_limit_bytes=58 * 1024 * 1024),
            cost_estimate=pl.CostEstimate(
                flops=28 * 2 * npairs * pix * chans * chans, bytes_accessed=10 * 2**20, transcendentals=0),
            name="block",
        )(inputs, temporal_weight, spatial, pooled_grad)
        input_grad, temporal_grad, spatial_grad = pl.pallas_call(
            write_out,
            out_shape=[
                jax.ShapeDtypeStruct(inputs.shape, BF16),
                jax.ShapeDtypeStruct((3, chans, chans), F32),
                jax.ShapeDtypeStruct((9, chans, chans), F32),
            ],
            in_specs=[pl.BlockSpec(memory_space=pl.ANY)] * 3,
            out_specs=[any_spec] * 3,
            scratch_shapes=[pltpu.SemaphoreType.DMA((nframes + 12,))],
            compiler_params=pltpu.CompilerParams(vmem_limit_bytes=2**20),
            name="write_out",
        )(input_grad, temporal_grad.reshape(3, chans, chans), spatial_grad.reshape(9, chans, chans))
        return input_grad, temporal_grad, spatial_grad.reshape(3, 3, chans, chans)

    in_specs = (P("frame", "row", None, None), P(), P(), P("frame", "row", None, None))
    out_specs = (P("frame", "row", None, None), P(), P())
    return jax.shard_map(body, mesh=mesh, in_specs=in_specs, out_specs=out_specs, check_vma=False)
```
